32 devices in a mesh: seq: 16 (over z, y, x), head: 2 (over core).
Axes of the slice: x: 2, y: 2, z: 4, core: 2. Of those that a mesh axis runs over, the one named last changes fastest.
Arguments:
- hidden_in: bfloat16 [8192, 2048], P('seq'), may hold values from -6 to 6
- cotangent: bfloat16 [8192, 2048], P('seq'), may hold values from -6 to 6
- lengths: int32 [3], replicated, may hold values from 1 to 62, as said below
- dealing: int32 [3], replicated, may hold values from 0 to 2, as said below
- norm_attn: float32 [2048], replicated, may hold values from 0.5 to 1.5
- w_query: bfloat16 [2048, 1024], P('seq', 'head'), may hold values from -0.125 to 0.125
- w_key: bfloat16 [2048, 1024], P('seq', 'head'), may hold values from -0.125 to 0.125
- w_value: bfloat16 [2048, 2048], P('seq', 'head'), may hold values from -0.125 to 0.125
- w_rank_in: bfloat16 [2048, 16], replicated, may hold values from -0.125 to 0.125
- w_rank_out: bfloat16 [16, 1024], P(None, 'head'), may hold values from -1.5 to 1.5
- decay_bias: float32 [1024], P('head'), may hold values from -1 to 10
- w_gate_out: bfloat16 [2048, 2048], P('seq', 'head'), may hold values from -0.125 to 0.125
- head_gain: float32 [512], replicated, may hold values from 0.5 to 1.5
- w_out: bfloat16 [2048, 2048], P('head', 'seq'), may hold values from -0.125 to 0.125
- norm_mlp: float32 [2048], replicated, may hold values from 0.5 to 1.5
- w_ff_gate: bfloat16 [2048, 5632], P('seq', 'head'), may hold values from -0.125 to 0.125
- w_ff_up: bfloat16 [2048, 5632], P('seq', 'head'), may hold values from -0.125 to 0.125
- w_ff_down: bfloat16 [5632, 2048], P('head', 'seq'), may hold values from -0.078125 to 0.078125
Outputs:
- block_out: bfloat16 [8192, 2048], P('seq')
- grad_input: float32 [8192, 2048], P('seq')
- grad_norm_attn: float32 [2048], replicated
- grad_query: float32 [2048, 1024], P('seq', 'head')
- grad_key: float32 [2048, 1024], P('seq', 'head')
- grad_value: float32 [2048, 2048], P('seq', 'head')
- grad_rank_in: float32 [2048, 16], replicated
- grad_rank_out: float32 [16, 1024], P(None, 'head')
- grad_decay_bias: float32 [1024], P('head')
- grad_gate_out: float32 [2048, 2048], P('seq', 'head')
- grad_head_gain: float32 [512], replicated
- grad_out_proj: float32 [2048, 2048], P('head', 'seq')
- grad_norm_mlp: float32 [2048], replicated
- grad_ff_gate: float32 [2048, 5632], P('seq', 'head')
- grad_ff_up: float32 [2048, 5632], P('seq', 'head')
- grad_ff_down: float32 [5632, 2048], P('head', 'seq')
The draws below stay inside these ranges and needn't reach their ends.
Inputs may be any that keep to these rules, and one draw needn't show every extreme that they name: lengths sum to 64; in packed order the first and the last sequence each have fewer than 4 blocks, so the middle one runs from the first device of seq to the last. `dealing`: a permutation of the sequence numbers.
All inputs are finite; a program needn't handle non-finite values.
Results may differ from the reference program's by a relative error of at most 0.0095.
The reference program's roundings to bfloat16 on the way count: a program that leaves them out, or rounds other values in their place, can miss the bound.
Values may be sent and summed in bfloat16 or wider, within the bound.
No kernel may reach another device: no remote copies, remote signals or barrier semaphores. Data moves between devices by JAX's collectives and lax.ppermute only.
A program may use at most 256 MiB of HBM per device.

```python
import jax
import jax.numpy as jnp
from jax import lax

D = 2048
HEADS = 4
DK = 256
DV = 512
FF = 5632
RANK = 16
SPAN = 64
BLOCK = 128
SEQUENCES = 3
TOK_DEV = 512
TOKENS = 8192
KEYS = 1024
VALS = 2048


def layout(key):
    order = jax.random.permutation(key, SEQUENCES).astype(jnp.int32)
    per_device = TOK_DEV // BLOCK
    total = TOKENS // BLOCK
    first = jax.random.randint(jax.random.fold_in(key, 11), (1,), 1, per_device).astype(jnp.int32)
    final = jax.random.randint(jax.random.fold_in(key, 13), (1,), 1, per_device).astype(jnp.int32)
    placed = jnp.concatenate([first, total - first - final, final]).astype(jnp.int32)
    return (order, placed)


def draw_dealing(key, part):
    order, placed = layout(key)
    return order


def draw_lengths(key, part):
    order, placed = layout(key)
    return jnp.zeros((SEQUENCES,), jnp.int32).at[order].set(placed)


def levels(own_key, extent, cuts, low, top_value):
    level, own = 1.0, jax.random.fold_in(own_key, 6)
    for dim, blocks in cuts:
        steps = jnp.exp(jax.random.uniform(jax.random.fold_in(own, dim), (blocks,), jnp.float32, low / len(cuts), top_value / len(cuts)))
        level = level * jnp.repeat(steps, extent[dim] // blocks).reshape([-1 if axis == dim else 1 for axis in range(len(extent))])
    return level


def noise(key, extent, spread, bound, cuts=(), kind=jnp.bfloat16):
    loudness = levels(key, extent, cuts, -0.22, 0.18) if cuts else 1.0
    values = jax.random.normal(key, extent, jnp.float32) * spread * loudness
    return jnp.minimum(jnp.maximum(values, -bound), bound).astype(kind)


def setup_inputs(seed: int = 0) -> dict:
    key_list = jax.random.split(jax.random.key(seed), 19)
    hidden_in = noise(key_list[0], (TOKENS, D), 1.0, 6.0, ((0, 16),))
    cotangent = noise(key_list[1], (TOKENS, D), 1.0, 6.0, ((0, 16),))
    lengths = draw_lengths(jax.random.fold_in(key_list[18], 71), 0)
    dealing = draw_dealing(jax.random.fold_in(key_list[18], 71), 0)
    norm_attn = jnp.clip(1.0 + 0.1 * jax.random.normal(key_list[4], (D,), jnp.float32), 0.5, 1.5)
    w_query = noise(key_list[5], (D, KEYS), D ** -0.5, 0.125, ((0, 16), (1, 2)))
    w_key = noise(key_list[6], (D, KEYS), D ** -0.5, 0.125, ((0, 16), (1, 2)))
    w_value = noise(key_list[7], (D, VALS), D ** -0.5, 0.125, ((0, 16), (1, 2)))
    w_rank_in = noise(key_list[8], (D, RANK), D ** -0.5, 0.125)
    w_rank_out = noise(key_list[9], (RANK, KEYS), RANK ** -0.5, 1.5, ((1, 2),))
    decay_bias = jnp.clip(-1.0 + 11.0 * jax.random.uniform(key_list[10], (KEYS,), jnp.float32) ** levels(key_list[10], (KEYS,), ((0, 2),), -0.2, 0.2), -1.0, 10.0)
    w_gate_out = noise(key_list[11], (D, VALS), D ** -0.5, 0.125, ((0, 16), (1, 2)))
    head_gain = jnp.clip(1.0 + 0.1 * jax.random.normal(key_list[12], (DV,), jnp.float32), 0.5, 1.5)
    w_out = noise(key_list[13], (VALS, D), VALS ** -0.5, 0.125, ((0, 2), (1, 16)))
    norm_mlp = jnp.clip(1.0 + 0.1 * jax.random.normal(key_list[14], (D,), jnp.float32), 0.5, 1.5)
    w_ff_gate = noise(key_list[15], (D, FF), D ** -0.5, 0.125, ((0, 16), (1, 2)))
    w_ff_up = noise(key_list[16], (D, FF), D ** -0.5, 0.125, ((0, 16), (1, 2)))
    w_ff_down = noise(key_list[17], (FF, D), FF ** -0.5, 0.078125, ((0, 2), (1, 16)))
    return {"hidden_in": hidden_in, "cotangent": cotangent, "lengths": lengths, "dealing": dealing, "norm_attn": norm_attn, "w_query": w_query, "w_key": w_key, "w_value": w_value, "w_rank_in": w_rank_in, "w_rank_out": w_rank_out, "decay_bias": decay_bias, "w_gate_out": w_gate_out, "head_gain": head_gain, "w_out": w_out, "norm_mlp": norm_mlp, "w_ff_gate": w_ff_gate, "w_ff_up": w_ff_up, "w_ff_down": w_ff_down}


EPSILON = 1e-06
HIGH_PRECISION = lax.Precision.HIGHEST

@jax.custom_vjp
def low(v):
    return lax.optimization_barrier(v.astype(jnp.bfloat16)).astype(jnp.float32)

@jax.custom_vjp
def low_back(v):
    return v

def low_keep(v):
    return (low(v), None)

def low_pass(kept, grad):
    return (grad,)

def back_keep(v):
    return (v, None)

def back_low(kept, grad):
    return (low(grad),)
low.defvjp(low_keep, low_pass)
low_back.defvjp(back_keep, back_low)

def rms_scale(value_columns, gain):
    return value_columns * lax.rsqrt(lax.optimization_barrier(jnp.mean(value_columns * value_columns, axis=-1, keepdims=True)) + EPSILON) * gain

def span_resets(lengths, dealing, count, start_span):
    number = lengths.shape[0]
    picks = (dealing[:, None] == jnp.arange(number, dtype=jnp.int32)[None, :]).astype(jnp.int32)
    placed = lax.optimization_barrier(jnp.sum(picks * lengths[None, :], axis=1, dtype=jnp.int32))
    ends = jnp.cumsum(placed, dtype=jnp.int32) * BLOCK
    starts = ends - placed * BLOCK
    firsts = (start_span + jnp.arange(count, dtype=jnp.int32)) * SPAN
    return jnp.any(firsts[:, None] == starts[None, :], axis=1).astype(jnp.float32)

def span_step(running_state, block):
    scaled, keys, value_columns, decay, reset = block
    running_state = running_state * (1.0 - reset)
    running = jnp.cumsum(decay, axis=0)
    query_decayed = scaled * jnp.exp(running)
    key_dec = keys * jnp.exp(-running)
    cross_block_term = jnp.einsum('xzt,ztw->xzw', query_decayed, running_state, precision=HIGH_PRECISION)
    scores = jnp.einsum('thk,shk->hts', query_decayed, key_dec, precision=HIGH_PRECISION)
    length = scaled.shape[0]
    lower = jnp.arange(length)[:, None] >= jnp.arange(length)[None, :]
    scores = jnp.where(lower[None], scores, 0.0)
    within = jnp.einsum('hts,shv->thv', scores, value_columns, precision=HIGH_PRECISION)
    closing_state = running[-1]
    key_tail_decay = keys * jnp.exp(closing_state[None] - running)
    running_state = jnp.exp(closing_state)[:, :, None] * running_state + jnp.einsum('jur,juo->uro', key_tail_decay, value_columns, precision=HIGH_PRECISION)
    return (running_state, cross_block_term + within)

def gla_run(scaled, keys, value_columns, decay, resets, running_state):
    running_state, outputs = lax.scan(jax.checkpoint(span_step), running_state, (scaled, keys, value_columns, decay, resets))
    return (outputs, running_state)

def forward(hidden, norm_attn, w_query, w_key, w_value, w_rank_in, w_rank_out, decay_bias, w_gate_out, head_gain, w_out, norm_mlp, w_ff_gate, w_ff_up, w_ff_down, resets):
    first_in = low(rms_scale(hidden, norm_attn))
    queries = low_back(jnp.dot(first_in, w_query, precision=HIGH_PRECISION))
    keys = low_back(jnp.dot(first_in, w_key, precision=HIGH_PRECISION))
    value_columns = low_back(jnp.dot(first_in, w_value, precision=HIGH_PRECISION))
    rank_in = low(jnp.dot(first_in, w_rank_in, precision=HIGH_PRECISION))
    logits = jnp.dot(rank_in, w_rank_out, precision=HIGH_PRECISION) + decay_bias
    log_decay = jax.nn.log_sigmoid(logits) / 16.0
    gate_pre = low_back(jnp.dot(first_in, w_gate_out, precision=HIGH_PRECISION))
    count = hidden.shape[0] // SPAN
    shape_key = (count, SPAN, HEADS, DK)
    outputs, ignored = gla_run((queries * DK ** (-0.5)).reshape(shape_key), keys.reshape(shape_key), value_columns.reshape(count, SPAN, HEADS, DV), log_decay.reshape(shape_key), resets, jnp.zeros((HEADS, DK, DV), jnp.float32))
    mixed_output = outputs.reshape(-1, HEADS, DV)
    normed = rms_scale(mixed_output, head_gain).reshape(-1, HEADS * DV)
    gated = low(normed * jax.nn.silu(gate_pre))
    attention = low_back(jnp.dot(gated, w_out, precision=HIGH_PRECISION))
    resid = hidden + attention
    second_in = low(rms_scale(resid, norm_mlp))
    ff_pre = low_back(jnp.dot(second_in, w_ff_gate, precision=HIGH_PRECISION))
    up_pre = low_back(jnp.dot(second_in, w_ff_up, precision=HIGH_PRECISION))
    inner = low(jax.nn.silu(ff_pre) * up_pre)
    branch = low_back(jnp.dot(inner, w_ff_down, precision=HIGH_PRECISION))
    return resid + branch

def reference(hidden_in, cotangent, lengths, dealing, norm_attn, w_query, w_key, w_value, w_rank_in, w_rank_out, decay_bias, w_gate_out, head_gain, w_out, norm_mlp, w_ff_gate, w_ff_up, w_ff_down):
    count = hidden_in.shape[0] // SPAN
    resets = span_resets(lengths, dealing, count, 0)

    def run(hidden, *weights):
        return forward(hidden, *weights, resets)
    params = (norm_attn.astype(jnp.float32), w_query.astype(jnp.float32), w_key.astype(jnp.float32), w_value.astype(jnp.float32), w_rank_in.astype(jnp.float32), w_rank_out.astype(jnp.float32), decay_bias.astype(jnp.float32), w_gate_out.astype(jnp.float32), head_gain.astype(jnp.float32), w_out.astype(jnp.float32), norm_mlp.astype(jnp.float32), w_ff_gate.astype(jnp.float32), w_ff_up.astype(jnp.float32), w_ff_down.astype(jnp.float32))
    result, pullback = jax.vjp(run, hidden_in.astype(jnp.float32), *params)
    grads = pullback(cotangent.astype(jnp.float32))
    return (result.astype(jnp.bfloat16), grads[0], grads[1], grads[2], grads[3], grads[4], grads[5], grads[6], grads[7], grads[8], grads[9], grads[10], grads[11], grads[12], grads[13], grads[14])
```

```python
import functools

import jax
import jax.numpy as jnp
from jax import lax
from jax.experimental import pallas as pl
from jax.experimental.pallas import tpu as pltpu
from jax.sharding import PartitionSpec as P

DK = 256
DV = 512
BLOCK = 128
HALF = BLOCK // 2
EPSILON = 1e-06
LOW = jnp.bfloat16
FULL = jnp.float32
LANES = 128

NN = ((1,), (0,))
TN = ((0,), (0,))
NT = ((1,), (1,))


def dot(left, right, dims=NN):
    return lax.dot_general(left, right, (dims, ((), ())), preferred_element_type=FULL)


def halves(x):
    high = x.astype(LOW)
    return high, (x - high.astype(FULL)).astype(LOW)


def thirds(x):
    high, rest = x.astype(LOW), None
    rest = x - high.astype(FULL)
    middle = rest.astype(LOW)
    return high, middle, (rest - middle.astype(FULL)).astype(LOW)


def fine(left, right, dims=NN):
    (lh, ll), (rh, rl) = left, right
    return dot(lh, rh, dims) + (dot(lh, rl, dims) + dot(ll, rh, dims))


def triangle(lower):
    row = lax.broadcasted_iota(jnp.int32, (BLOCK, BLOCK), 0)
    col = lax.broadcasted_iota(jnp.int32, (BLOCK, BLOCK), 1)
    return row >= col if lower else row <= col


def running_sum(x, lower=True):
    ones = triangle(lower).astype(FULL).astype(LOW)
    high, middle, low = thirds(x)
    return dot(ones, high) + (dot(ones, middle) + dot(ones, low))


def column_sum(x):
    ones = jnp.ones((x.shape[0], LANES), LOW)
    high, middle, low = thirds(x)
    return dot(high, ones, TN) + (dot(middle, ones, TN) + dot(low, ones, TN))


def widen(column, width):
    return jnp.concatenate([column] * (width // LANES), axis=1)


def summary_kernel(info, k_ref, v_ref, decay_ref, out_ref, state, passed, total):
    step, count = pl.program_id(0), pl.num_programs(0)
    at = count - 1 - step

    @pl.when(step == 0)
    def _():
        state[...] = jnp.zeros_like(state)
        passed[...] = jnp.zeros_like(passed)
        total[...] = jnp.zeros_like(total)

    decay = decay_ref[...]
    run = running_sum(decay)
    closing = run[BLOCK - 1 :, :]
    alive = info[1 + count + at].astype(FULL)
    tail = jnp.exp(passed[0:1, :] + closing - run) * (k_ref[...] * alive)
    state[...] += fine(halves(tail), halves(v_ref[...]), TN)
    passed[0:1, :] += closing
    total[...] += column_sum(decay)

    @pl.when(step == count - 1)
    def _():
        out_ref[:, :DV] = state[...]
        out_ref[:, DV:] = jnp.exp(total[...]) * info[1 + 3 * count].astype(FULL)


def mix_kernel(
    info, q_ref, k_ref, v_ref, g_ref, decay_ref, enter_ref, gain_ref, mixed_ref, gated_ref, states_ref, state
):
    step = pl.program_id(0)

    @pl.when(step == 0)
    def _():
        state[...] = enter_ref[...]

    begin = jnp.where(info[1 + step] > 0, jnp.zeros_like(state), state[...])
    states_ref[0] = begin
    decay = decay_ref[...]
    run = running_sum(decay)
    middle, closing = run[HALF - 1 : HALF, :], run[BLOCK - 1 :, :]
    q = q_ref[...] * DK ** (-0.5)
    k = k_ref[...]
    v = halves(v_ref[...])
    near_q, near_k = halves(q * jnp.exp(run - middle)), halves(k * jnp.exp(middle - run))
    scores = jnp.where(triangle(True), fine(near_q, near_k, NT), 0.0)
    out = fine(halves(q * jnp.exp(run)), halves(begin)) + fine(halves(scores), v)
    tail = halves(k * jnp.exp(closing - run))
    state[...] = widen(jnp.exp(column_sum(decay)), DV) * begin + fine(tail, v, TN)
    mixed_ref[...] = out
    normed = out * lax.rsqrt(jnp.mean(out * out, axis=1, keepdims=True) + EPSILON) * gain_ref[...]
    gate = g_ref[...]
    gated_ref[...] = (normed * (gate * jax.nn.sigmoid(gate))).astype(LOW)


def gate_back_kernel(
    info, q_ref, g_ref, decay_ref, mixed_ref, grad_ref, gain_ref, back_ref, dmixed_ref, out_ref, dgain_ref, state, passed
):
    step, count = pl.program_id(0), pl.num_programs(0)

    @pl.when(step == 0)
    def _():
        state[...] = jnp.zeros_like(state)
        passed[...] = jnp.zeros_like(passed)
        dgain_ref[...] = jnp.zeros_like(dgain_ref)

    mixed, gate, grad, gain = mixed_ref[...], g_ref[...], grad_ref[...], gain_ref[...]
    scale = lax.rsqrt(jnp.mean(mixed * mixed, axis=1, keepdims=True) + EPSILON)
    normed = mixed * scale
    soft = jax.nn.sigmoid(gate)
    back_ref[...] = (grad * (normed * gain) * (soft * (1.0 + gate * (1.0 - soft)))).astype(LOW)
    error = grad * (gate * soft)
    dgain_ref[...] += jnp.sum(error * normed, axis=0, keepdims=True)
    scaled = error * gain
    dmixed = scale * (scaled - normed * jnp.mean(scaled * normed, axis=1, keepdims=True))
    dmixed_ref[...] = dmixed
    run = running_sum(decay_ref[...])
    alive = info[1 + 2 * count + step].astype(FULL)
    reach = jnp.exp(passed[0:1, :] + run) * (q_ref[...] * (DK ** (-0.5) * alive))
    state[...] += fine(halves(reach), halves(dmixed), TN)
    passed[0:1, :] += run[BLOCK - 1 :, :]

    @pl.when(step == count - 1)
    def _():
        out_ref[...] = state[...]


def mix_back_kernel(
    info,
    q_ref,
    k_ref,
    v_ref,
    decay_ref,
    logits_ref,
    states_ref,
    dmixed_ref,
    gate_ref,
    leave_ref,
    back_ref,
    dlogits_ref,
    dbias_ref,
    state,
):
    step, count = pl.program_id(0), pl.num_programs(0)
    at = count - 1 - step

    @pl.when(step == 0)
    def _():
        state[...] = leave_ref[...]
        dbias_ref[...] = jnp.zeros_like(dbias_ref)

    after, begin = state[...], states_ref[0]
    decay = decay_ref[...]
    run = running_sum(decay)
    middle, closing = run[HALF - 1 : HALF, :], run[BLOCK - 1 :, :]
    q, k = q_ref[...] * DK ** (-0.5), k_ref[...]
    grow, shrink = jnp.exp(run - middle), jnp.exp(middle - run)
    from_start, to_end = jnp.exp(run), jnp.exp(closing - run)
    near_q, near_k = halves(q * grow), halves(k * shrink)
    v, dout = halves(v_ref[...]), halves(dmixed_ref[...])
    after_parts = halves(after)
    keep = triangle(True)
    scores = halves(jnp.where(keep, fine(near_q, near_k, NT), 0.0))
    dscores = halves(jnp.where(keep, fine(dout, v, NT), 0.0))
    tail = k * to_end
    dtail = fine(v, after_parts, NT)
    dq = fine(dscores, near_k) * grow + fine(dout, halves(begin), NT) * from_start
    dk = fine(dscores, near_q, TN) * shrink + dtail * to_end
    dv = fine(scores, dout, TN) + fine(halves(tail), after_parts)
    ones = jnp.ones((16, DV), LOW)
    high, low = halves(begin * after)
    across = (dot(ones, high, NT) + dot(ones, low, NT))[0:1, :]
    dclosing = jnp.sum(dtail * tail, axis=0, keepdims=True) + jnp.exp(closing) * across
    ddecay = running_sum(dq * q - dk * k, lower=False) + dclosing
    dlogits = ddecay * jax.nn.sigmoid(-logits_ref[...]) * (1.0 / 16.0)
    dlogits_ref[...] = dlogits
    dbias_ref[...] += jnp.sum(dlogits, axis=0, keepdims=True)
    back_ref[:, :DK] = (dq * DK ** (-0.5)).astype(LOW)
    back_ref[:, DK : 2 * DK] = dk.astype(LOW)
    back_ref[:, 2 * DK : 2 * DK + DV] = dv.astype(LOW)
    back_ref[:, 2 * DK + DV :] = gate_ref[...]
    before = widen(jnp.exp(column_sum(decay)), DV) * after + fine(halves(q * from_start), dout, TN)
    state[...] = jnp.where(info[1 + at] > 0, jnp.zeros_like(before), before)


PARAMS = pltpu.CompilerParams(
    dimension_semantics=("arbitrary",), vmem_limit_bytes=40 * 1024 * 1024
)


def token_call(kernel, info, count, quarter, reverse, inputs, outputs, scratch, flops):
    per = quarter // BLOCK

    def place(i):
        return count - 1 - i if reverse else i

    def spec(shape, column):
        if column is None:
            return pl.BlockSpec(shape, lambda i, info: (0, 0))
        if column == "state":
            return pl.BlockSpec(shape, lambda i, info: (place(i), 0, 0))

        def index(i, info):
            j = place(i)
            return ((j // per) ^ info[0]) * per + j % per, column

        return pl.BlockSpec(shape, index)

    return pl.pallas_call(
        kernel,
        grid_spec=pltpu.PrefetchScalarGridSpec(
            num_scalar_prefetch=1,
            grid=(count,),
            in_specs=[spec(shape, column) for _, shape, column in inputs],
            out_specs=[spec(shape, column) for _, shape, column in outputs],
            scratch_shapes=scratch,
        ),
        out_shape=[out for out, _, _ in outputs],
        compiler_params=PARAMS,
        cost_estimate=pl.CostEstimate(flops=flops, bytes_accessed=1 << 24, transcendentals=1 << 20),
    )(info, *[array for array, _, _ in inputs])


def shape_of(*extent, dtype=FULL):
    return jax.ShapeDtypeStruct(extent, dtype)


def columns_in_kernel(order, core, a, b, c, d, oa, ob, oc, od):
    oa[...] = a[...]
    ob[...] = b[...]
    oc[...] = c[...]
    od[...] = d[...]


def columns_in(hidden, cotangent, gain_a, gain_b, order, core, quarter, wide):
    count = order.shape[0]
    if wide % LANES:
        def pick(x):
            return jnp.concatenate(
                [lax.dynamic_slice_in_dim(x, order[i] * wide, wide, 1) for i in range(count)], axis=1
            )

        def rows(x):
            return lax.dynamic_slice_in_dim(x, core * quarter, quarter, 0)

        return pick(rows(hidden)), pick(rows(cotangent)), pick(gain_a), pick(gain_b)
    big = pl.BlockSpec((quarter, wide), lambda i, order, core: (core[0], order[i]))
    small = pl.BlockSpec((1, wide), lambda i, order, core: (0, order[i]))
    big_out = pl.BlockSpec((quarter, wide), lambda i, order, core: (0, i))
    small_out = pl.BlockSpec((1, wide), lambda i, order, core: (0, i))
    total = count * wide
    return pl.pallas_call(
        columns_in_kernel,
        grid_spec=pltpu.PrefetchScalarGridSpec(
            num_scalar_prefetch=2,
            grid=(count,),
            in_specs=[big, big, small, small],
            out_specs=[big_out, big_out, small_out, small_out],
        ),
        out_shape=[
            shape_of(quarter, total, dtype=LOW),
            shape_of(quarter, total, dtype=LOW),
            shape_of(1, total),
            shape_of(1, total),
        ],
        compiler_params=PARAMS,
    )(order, core.reshape(1), hidden, cotangent, gain_a, gain_b)


def columns_out_kernel(order, core, mine, near, out):
    quarter = mine.shape[0]
    first = core[0] == 0
    out[:quarter, :] = jnp.where(first, mine[...], near[...])
    out[quarter:, :] = jnp.where(first, near[...], mine[...])


def columns_out(mine, near, order, inverse, core, wide):
    quarter, total = mine.shape
    count = order.shape[0]
    if wide % LANES:
        first = core == 0
        both = jnp.concatenate([jnp.where(first, mine, near), jnp.where(first, near, mine)], axis=0)
        return jnp.concatenate(
            [lax.dynamic_slice_in_dim(both, inverse[i] * wide, wide, 1) for i in range(count)], axis=1
        )
    spec = pl.BlockSpec((quarter, wide), lambda i, order, core: (0, i))
    return pl.pallas_call(
        columns_out_kernel,
        grid_spec=pltpu.PrefetchScalarGridSpec(
            num_scalar_prefetch=2,
            grid=(count,),
            in_specs=[spec, spec],
            out_specs=pl.BlockSpec((2 * quarter, wide), lambda i, order, core: (0, order[i])),
        ),
        out_shape=shape_of(2 * quarter, total, dtype=mine.dtype),
        compiler_params=PARAMS,
    )(order, core.reshape(1), mine, near)


def block_resets(lengths, dealing, count, start):
    number = lengths.shape[0]
    picks = (dealing[:, None] == jnp.arange(number, dtype=jnp.int32)[None, :]).astype(jnp.int32)
    placed = jnp.sum(picks * lengths[None, :], axis=1, dtype=jnp.int32)
    ends = jnp.cumsum(placed, dtype=jnp.int32)
    starts = ends - placed
    firsts = start + jnp.arange(count, dtype=jnp.int32)
    return jnp.any(firsts[:, None] == starts[None, :], axis=1).astype(jnp.int32)


def tied(*values):
    return lax.optimization_barrier(values)


def silu(x):
    return x * jax.nn.sigmoid(x)


def shards(
    hidden_in,
    cotangent,
    lengths,
    dealing,
    norm_attn,
    w_query,
    w_key,
    w_value,
    w_rank_in,
    w_rank_out,
    decay_bias,
    w_gate_out,
    head_gain,
    w_out,
    norm_mlp,
    w_ff_gate,
    w_ff_up,
    w_ff_down,
):
    peers = lax.axis_size("seq")
    place, core = lax.axis_index("seq"), lax.axis_index("head")
    laps, groups = peers // 4, peers // 2
    group, left = place // 2, place % 2 == 0
    rows, width = hidden_in.shape
    quarter = rows // 2
    tokens = 4 * quarter
    count = tokens // BLOCK
    wide = width // groups
    ff = w_ff_gate.shape[1] // 2

    def pair(x):
        return lax.ppermute(x, "seq", [(i, i ^ 1) for i in range(peers)])

    def side(x):
        return lax.ppermute(x, "seq", [(i, i ^ 2) for i in range(peers)])

    def ring(x):
        return lax.ppermute(x, "seq", [(i, (i + 4) % peers) for i in range(peers)])

    def twin(x):
        return lax.ppermute(x, "head", [(0, 1), (1, 0)])

    lap, flank = group // 2, group % 2
    steps = jnp.arange(groups, dtype=jnp.int32)
    order = ((lap - steps % laps) % laps) * 2 + (flank ^ (steps // laps))
    inverse = (flank ^ (steps % 2)) * laps + (lap - steps // 2) % laps
    resets = block_resets(lengths, dealing, count, group * count)
    ahead = jnp.cumsum(resets)
    info = jnp.concatenate(
        [
            ((place % 2) * 2 + core).astype(jnp.int32).reshape(1),
            resets,
            (ahead == ahead[-1]).astype(jnp.int32),
            (ahead == 0).astype(jnp.int32),
            (ahead[-1:] == 0).astype(jnp.int32),
        ]
    )

    def split(*arrays):
        mid = [a.shape[1] // 2 for a in arrays]
        low = jnp.concatenate([a[:, :m] for a, m in zip(arrays, mid)], axis=1)
        high = jnp.concatenate([a[:, m:] for a, m in zip(arrays, mid)], axis=1)
        return jnp.where(left, low, high), jnp.where(left, high, low)

    def exchanged(mine, other):
        got = pair(other)
        return jnp.concatenate(
            [jnp.where(left, mine, got), jnp.where(left, got, mine)], axis=0
        )

    def collected(own, after):
        if after is not None:
            own, _ = tied(own, after)
        blocks, others = [own], []
        for step in range(laps):
            if step < laps - 1:
                new, other = tied(ring(blocks[-1]), side(blocks[-1]))
                blocks.append(new)
                others.append(other)
            else:
                others.append(side(blocks[-1]))
        return jnp.concatenate(blocks + others, axis=0), blocks[-1]

    mine_q, other_q = split(w_query, w_key, w_value, w_gate_out)
    mine_o, other_o = split(w_out.T)
    mine_f, other_f = split(w_ff_gate, w_ff_up)
    mine_d, other_d = split(w_ff_down.T)
    pair_q = exchanged(mine_q, other_q)

    hidden_low, cot_own, gain_attn, gain_mlp = columns_in(
        hidden_in, cotangent, norm_attn[None], norm_mlp[None], order, core, quarter, wide
    )
    rank_weight = jnp.concatenate(
        [lax.dynamic_slice_in_dim(w_rank_in, order[i] * wide, wide, 0) for i in range(groups)], axis=0
    )

    def spread(x):
        near, far = twin(x), pair(x)
        return jnp.concatenate([x, near, far, twin(far)], axis=0)

    def gathered_sum(parts):
        q = quarter
        far = parts[2 * q : 3 * q] + twin(parts[3 * q :].astype(LOW))
        got = pair(far.astype(LOW))
        return parts[:q] + twin(parts[q : 2 * q].astype(LOW)) + got

    hidden = hidden_low.astype(FULL)
    scale_attn = lax.rsqrt(jnp.mean(hidden * hidden, axis=1, keepdims=True) + EPSILON)
    first = spread((hidden * scale_attn * gain_attn).astype(LOW))

    full_q, done = collected(pair_q, None)
    other_o, other_f, other_d, _ = tied(other_o, other_f, other_d, first)
    pair_o, pair_f, pair_d = (
        exchanged(mine_o, other_o),
        exchanged(mine_f, other_f),
        exchanged(mine_d, other_d),
    )
    full_o, done = collected(pair_o, done)
    full_f, done = collected(pair_f, done)
    full_d, done = collected(pair_d, done)

    mixes = dot(first, full_q)
    rank_in = dot(first, rank_weight).astype(LOW)
    rank_out = jnp.where(left, w_rank_out[:, :DK], w_rank_out[:, DK:])
    bias = jnp.where(left, decay_bias[:DK], decay_bias[DK:])
    logits = dot(rank_in, rank_out) + bias
    decay = jax.nn.log_sigmoid(logits) / 16.0
    gain = head_gain[None]
    state_scratch = pltpu.VMEM((DK, DV), FULL)
    row_scratch = pltpu.VMEM((8, DK), FULL)
    key_block, val_block = (BLOCK, DK), (BLOCK, DV)
    state_shape = (DK, DV)
    call = functools.partial(token_call, info=info, count=count, quarter=quarter)
    (summary,) = call(
        summary_kernel,
        reverse=True,
        inputs=[(mixes, key_block, 1), (mixes, val_block, 1), (decay, key_block, 0)],
        outputs=[(shape_of(DK, DV + LANES), (DK, DV + LANES), None)],
        scratch=[state_scratch, row_scratch, pltpu.VMEM((DK, LANES), FULL)],
        flops=1 << 30,
    )
    halves_of_seq = [[i for i in range(peers) if i % 2 == k] for k in range(2)]
    slab = DK // groups

    def turned(x):
        return lax.all_to_all(x, "seq", 0, 0, axis_index_groups=halves_of_seq, tiled=True)

    pieces = turned(summary).reshape(groups, slab, DV + LANES)
    through = pieces[:, :, DV : DV + 1]

    def carried(local, backwards):
        current, out = jnp.zeros((slab, DV), FULL), [None] * groups
        for j in reversed(range(groups)) if backwards else range(groups):
            out[j] = current
            current = through[j] * current + local[j]
        return turned(jnp.concatenate(out, axis=0))

    entering = carried(pieces[:, :, :DV], False)
    mixed, gated, states = call(
        mix_kernel,
        reverse=False,
        inputs=[
            (mixes, key_block, 0),
            (mixes, key_block, 1),
            (mixes, val_block, 1),
            (mixes, val_block, 2),
            (decay, key_block, 0),
            (entering, state_shape, None),
            (gain, (1, DV), None),
        ],
        outputs=[
            (shape_of(tokens, DV), val_block, 0),
            (shape_of(tokens, DV, dtype=LOW), val_block, 0),
            (shape_of(count, DK, DV), (1, DK, DV), "state"),
        ],
        scratch=[state_scratch],
        flops=3 << 30,
    )
    resid = hidden + gathered_sum(dot(gated, full_o, NT))
    scale_mlp = lax.rsqrt(jnp.mean(resid * resid, axis=1, keepdims=True) + EPSILON)
    second = spread((resid * scale_mlp * gain_mlp).astype(LOW))
    ff_both = dot(second, full_f)
    ff_pre, up_pre = ff_both[:, :ff], ff_both[:, ff:]
    inner = (silu(ff_pre) * up_pre).astype(LOW)
    cot_own, _ = tied(cot_own, done)
    cot = spread(cot_own)

    def reduced(tokens_left, tokens_right):
        def part(k):
            return dot(tokens_left[:, k * wide : (k + 1) * wide], tokens_right, TN)

        turn = [(p + 1) % laps for p in range(laps)]
        sent = {p: side(part(laps + p).astype(LOW)) for p in turn}
        own = {p: part(p) + sent[p] for p in turn}
        current = own[turn[0]]
        for p in turn[1:]:
            current = own[p] + ring(current.astype(LOW))
        high, low = current[: wide // 2], current[wide // 2 :]
        mine = jnp.where(left, high, low)
        got = pair(jnp.where(left, low, high).astype(LOW)).astype(FULL)
        return jnp.where(left, mine, got), jnp.where(left, got, mine)

    down_halves = reduced(cot, inner)
    out_own = (resid + gathered_sum(dot(inner, full_d, NT))).astype(LOW)
    block_out = columns_out(out_own, twin(out_own), order, inverse, core, wide)

    grad_inner = dot(cot, full_d)
    soft = jax.nn.sigmoid(ff_pre)
    ff_back = (grad_inner * up_pre * (soft * (1.0 + ff_pre * (1.0 - soft)))).astype(LOW)
    up_back = (grad_inner * (ff_pre * soft)).astype(LOW)
    both_back = jnp.concatenate([ff_back, up_back], axis=1)
    grad_second = gathered_sum(dot(both_back, full_f, NT))
    gate_halves = reduced(second, both_back[:, :ff])
    up_halves = reduced(second, both_back[:, ff:])

    def norm_back(grad, value, scale, gains):
        normed = value * scale
        scaled = grad * gains
        gain_grad = jnp.sum(grad * normed, axis=0, keepdims=True)
        return scale * (scaled - normed * jnp.mean(scaled * normed, axis=1, keepdims=True)), gain_grad

    resid_norm, grad_gain_mlp = norm_back(grad_second, resid, scale_mlp, gain_mlp)
    grad_resid = cot_own.astype(FULL) + resid_norm
    resid_back = spread(grad_resid.astype(LOW))
    grad_gated = dot(resid_back, full_o)
    gate_back, dmixed, summary_back, grad_gain_head = call(
        gate_back_kernel,
        reverse=False,
        inputs=[
            (mixes, key_block, 0),
            (mixes, val_block, 2),
            (decay, key_block, 0),
            (mixed, val_block, 0),
            (grad_gated, val_block, 0),
            (gain, (1, DV), None),
        ],
        outputs=[
            (shape_of(tokens, DV, dtype=LOW), val_block, 0),
            (shape_of(tokens, DV), val_block, 0),
            (shape_of(DK, DV), state_shape, None),
            (shape_of(1, DV), (1, DV), None),
        ],
        scratch=[state_scratch, row_scratch],
        flops=1 << 30,
    )
    out_halves = reduced(resid_back, gated)
    leaving = carried(turned(summary_back).reshape(groups, slab, DV), True)
    mixes_back, grad_logits, grad_bias = call(
        mix_back_kernel,
        reverse=True,
        inputs=[
            (mixes, key_block, 0),
            (mixes, key_block, 1),
            (mixes, val_block, 1),
            (decay, key_block, 0),
            (logits, key_block, 0),
            (states, (1, DK, DV), "state"),
            (dmixed, val_block, 0),
            (gate_back, val_block, 0),
            (leaving, state_shape, None),
        ],
        outputs=[
            (shape_of(tokens, mixes.shape[1], dtype=LOW), (BLOCK, mixes.shape[1]), 0),
            (shape_of(tokens, DK), key_block, 0),
            (shape_of(1, DK), (1, DK), None),
        ],
        scratch=[state_scratch],
        flops=8 << 30,
    )
    mix_halves = reduced(first, mixes_back)
    precise = lax.Precision.HIGHEST
    grad_rank_out = lax.dot_general(
        rank_in.astype(FULL), grad_logits, (TN, ((), ())), precision=precise
    )
    grad_rank = lax.dot_general(
        grad_logits, rank_out.astype(FULL), (NT, ((), ())), precision=precise
    )
    rank_high = grad_rank.astype(LOW)
    rank_low = (grad_rank - rank_high.astype(FULL)).astype(LOW)
    first_parts = dot(mixes_back, full_q, NT) + (
        dot(rank_high, rank_weight, NT) + dot(rank_low, rank_weight, NT)
    )
    grad_rank_in = dot(rank_high, first, TN) + dot(rank_low, first, TN)
    grad_first = gathered_sum(first_parts)
    hidden_norm, grad_gain_attn = norm_back(grad_first, hidden, scale_attn, gain_attn)
    input_own = grad_resid + hidden_norm
    grad_input = columns_out(input_own, twin(input_own), order, inverse, core, wide)

    def unordered(x):
        return jnp.concatenate(
            [lax.dynamic_slice_in_dim(x, inverse[i] * wide, wide, 1) for i in range(groups)], axis=1
        )

    wide_part = jnp.concatenate(
        [grad_rank_in, grad_gain_attn, grad_gain_mlp, jnp.zeros((6, width), FULL)], axis=0
    )
    wide_part = unordered(wide_part + twin(wide_part))
    empty = jnp.zeros_like(grad_rank_out)
    rank_part = jnp.concatenate(
        [jnp.where(left, grad_rank_out, empty), jnp.where(left, empty, grad_rank_out)], axis=1
    )
    bias_part = jnp.concatenate(
        [jnp.where(left, grad_bias, 0.0), jnp.where(left, 0.0, grad_bias)], axis=1
    )
    head_part = grad_gain_head + twin(grad_gain_head)
    narrow_part = jnp.concatenate(
        [rank_part, bias_part, head_part, jnp.zeros((6, 2 * DK), FULL)], axis=0
    )
    small = jnp.concatenate([wide_part, narrow_part], axis=1)
    hop = 1
    while hop < peers:
        small = small + lax.ppermute(small, "seq", [(i, i ^ hop) for i in range(peers)])
        hop *= 2

    def beside(pieces, start, stop):
        return jnp.concatenate([half[:, start:stop] for half in pieces], axis=1)

    return (
        block_out,
        grad_input,
        small[16, :width],
        beside(mix_halves, 0, DK),
        beside(mix_halves, DK, 2 * DK),
        beside(mix_halves, 2 * DK, 2 * DK + DV),
        small[:16, :width].T,
        small[:16, width:],
        small[16, width:],
        beside(mix_halves, 2 * DK + DV, 2 * DK + 2 * DV),
        small[17, width:],
        jnp.concatenate(out_halves, axis=1).T,
        small[17, :width],
        jnp.concatenate(gate_halves, axis=1),
        jnp.concatenate(up_halves, axis=1),
        jnp.concatenate(down_halves, axis=1).T,
    )


def solution(mesh):
    return jax.shard_map(
        shards,
        mesh=mesh,
        in_specs=(
            P("seq", None),
            P("seq", None),
            P(),
            P(),
            P(),
            P("seq", "head"),
            P("seq", "head"),
            P("seq", "head"),
            P(),
            P(None, "head"),
            P("head"),
            P("seq", "head"),
            P(),
            P("head", "seq"),
            P(),
            P("seq", "head"),
            P("seq", "head"),
            P("head", "seq"),
        ),
        out_specs=(
            P("seq", None),
            P("seq", None),
            P(),
            P("seq", "head"),
            P("seq", "head"),
            P("seq", "head"),
            P(),
            P(None, "head"),
            P("head"),
            P("seq", "head"),
            P(),
            P("head", "seq"),
            P(),
            P("seq", "head"),
            P("seq", "head"),
            P("head", "seq"),
        ),
        check_vma=False,
    )
```

```python
import functools

import jax
import jax.numpy as jnp
from jax import lax
from jax.experimental import pallas as pl
from jax.experimental.layout import Layout, with_layout_constraint
from jax.experimental.pallas import tpu as pltpu
from jax.sharding import PartitionSpec as P

DK = 256
DV = 512
BLOCK = 128
HALF = BLOCK // 2
EPSILON = 1e-06
LOW = jnp.bfloat16
FULL = jnp.float32
LANES = 128

NN = ((1,), (0,))
TN = ((0,), (0,))
NT = ((1,), (1,))


def dot(left, right, dims=NN):
    return lax.dot_general(left, right, (dims, ((), ())), preferred_element_type=FULL)


def halves(x):
    high = x.astype(LOW)
    return high, (x - high.astype(FULL)).astype(LOW)


def thirds(x):
    high, rest = x.astype(LOW), None
    rest = x - high.astype(FULL)
    middle = rest.astype(LOW)
    return high, middle, (rest - middle.astype(FULL)).astype(LOW)


def fine(left, right, dims=NN):
    (lh, ll), (rh, rl) = left, right
    return dot(lh, rh, dims) + (dot(lh, rl, dims) + dot(ll, rh, dims))


def triangle(lower):
    row = lax.broadcasted_iota(jnp.int32, (BLOCK, BLOCK), 0)
    col = lax.broadcasted_iota(jnp.int32, (BLOCK, BLOCK), 1)
    return row >= col if lower else row <= col


def running_sum(x, lower=True):
    ones = triangle(lower).astype(FULL).astype(LOW)
    high, middle, low = thirds(x)
    return dot(ones, high) + (dot(ones, middle) + dot(ones, low))


def column_sum(x):
    ones = jnp.ones((x.shape[0], LANES), LOW)
    high, middle, low = thirds(x)
    return dot(high, ones, TN) + (dot(middle, ones, TN) + dot(low, ones, TN))


def widen(column, width):
    return jnp.concatenate([column] * (width // LANES), axis=1)


def summary_kernel(info, k_ref, v_ref, decay_ref, out_ref, state, passed, total):
    step, count = pl.program_id(0), pl.num_programs(0)
    at = count - 1 - step

    @pl.when(step == 0)
    def _():
        state[...] = jnp.zeros_like(state)
        passed[...] = jnp.zeros_like(passed)
        total[...] = jnp.zeros_like(total)

    decay = decay_ref[...]
    run = running_sum(decay)
    closing = run[BLOCK - 1 :, :]
    alive = info[1 + count + at].astype(FULL)
    tail = jnp.exp(passed[0:1, :] + closing - run) * (k_ref[...] * alive)
    state[...] += fine(halves(tail), halves(v_ref[...]), TN)
    passed[0:1, :] += closing
    total[...] += column_sum(decay)

    @pl.when(step == count - 1)
    def _():
        out_ref[:, :DV] = state[...].astype(LOW)
        lane = lax.broadcasted_iota(jnp.int32, (DK, LANES), 1)
        high, middle, low = thirds(jnp.exp(total[...]) * info[1 + 3 * count].astype(FULL))
        high, middle, low = high.astype(FULL), middle.astype(FULL), low.astype(FULL)
        out_ref[:, DV:] = jnp.where(lane == 0, high, jnp.where(lane == 1, middle, low)).astype(LOW)


def chain_kernel(backwards, pieces_ref, local_ref, out_ref):
    groups, slab = local_ref.shape[0], local_ref.shape[1]
    current = jnp.zeros((slab, DV), FULL)
    for j in reversed(range(groups)) if backwards else range(groups):
        out_ref[j] = current.astype(LOW)
        through = pieces_ref[j][:, DV:].astype(FULL)
        through = through[:, 0:1] + through[:, 1:2] + through[:, 2:3]
        current = through * current + local_ref[j][:, :DV].astype(FULL)


def chain_call(pieces, local, backwards):
    groups, slab, _ = pieces.shape
    return pl.pallas_call(
        functools.partial(chain_kernel, backwards),
        out_shape=shape_of(groups, slab, DV, dtype=LOW),
        compiler_params=pltpu.CompilerParams(vmem_limit_bytes=40 * 1024 * 1024),
    )(pieces, local)


def mix_kernel(
    info, q_ref, k_ref, v_ref, g_ref, decay_ref, enter_ref, gain_ref, mixed_ref, gated_ref, states_ref, state
):
    step = pl.program_id(0)

    @pl.when(step == 0)
    def _():
        state[...] = enter_ref[...].astype(FULL)

    begin = jnp.where(info[1 + step] > 0, jnp.zeros_like(state), state[...])
    states_ref[0] = begin
    decay = decay_ref[...]
    run = running_sum(decay)
    middle, closing = run[HALF - 1 : HALF, :], run[BLOCK - 1 :, :]
    q = q_ref[...] * DK ** (-0.5)
    k = k_ref[...]
    v = halves(v_ref[...])
    near_q, near_k = halves(q * jnp.exp(run - middle)), halves(k * jnp.exp(middle - run))
    scores = jnp.where(triangle(True), fine(near_q, near_k, NT), 0.0)
    out = fine(halves(q * jnp.exp(run)), halves(begin)) + fine(halves(scores), v)
    tail = halves(k * jnp.exp(closing - run))
    state[...] = widen(jnp.exp(column_sum(decay)), DV) * begin + fine(tail, v, TN)
    mixed_ref[...] = out
    normed = out * lax.rsqrt(jnp.mean(out * out, axis=1, keepdims=True) + EPSILON) * gain_ref[...]
    gate = g_ref[...]
    gated_ref[...] = (normed * (gate * jax.nn.sigmoid(gate))).astype(LOW)


def gate_back_kernel(
    info, q_ref, g_ref, decay_ref, mixed_ref, grad_ref, gain_ref, back_ref, dmixed_ref, out_ref, dgain_ref, state, passed
):
    step, count = pl.program_id(0), pl.num_programs(0)

    @pl.when(step == 0)
    def _():
        state[...] = jnp.zeros_like(state)
        passed[...] = jnp.zeros_like(passed)
        dgain_ref[...] = jnp.zeros_like(dgain_ref)

    mixed, gate, grad, gain = mixed_ref[...], g_ref[...], grad_ref[...], gain_ref[...]
    scale = lax.rsqrt(jnp.mean(mixed * mixed, axis=1, keepdims=True) + EPSILON)
    normed = mixed * scale
    soft = jax.nn.sigmoid(gate)
    back_ref[...] = (grad * (normed * gain) * (soft * (1.0 + gate * (1.0 - soft)))).astype(LOW)
    error = grad * (gate * soft)
    dgain_ref[...] += jnp.sum(error * normed, axis=0, keepdims=True)
    scaled = error * gain
    dmixed = scale * (scaled - normed * jnp.mean(scaled * normed, axis=1, keepdims=True))
    dmixed_ref[...] = dmixed
    run = running_sum(decay_ref[...])
    alive = info[1 + 2 * count + step].astype(FULL)
    reach = jnp.exp(passed[0:1, :] + run) * (q_ref[...] * (DK ** (-0.5) * alive))
    state[...] += fine(halves(reach), halves(dmixed), TN)
    passed[0:1, :] += run[BLOCK - 1 :, :]

    @pl.when(step == count - 1)
    def _():
        out_ref[...] = state[...].astype(LOW)


def mix_back_kernel(
    info,
    q_ref,
    k_ref,
    v_ref,
    decay_ref,
    logits_ref,
    states_ref,
    dmixed_ref,
    leave_ref,
    back_ref,
    dlogits_ref,
    dbias_ref,
    state,
):
    step, count = pl.program_id(0), pl.num_programs(0)
    at = count - 1 - step

    @pl.when(step == 0)
    def _():
        state[...] = leave_ref[...].astype(FULL)
        dbias_ref[...] = jnp.zeros_like(dbias_ref)

    after, begin = state[...], states_ref[0]
    decay = decay_ref[...]
    run = running_sum(decay)
    middle, closing = run[HALF - 1 : HALF, :], run[BLOCK - 1 :, :]
    q, k = q_ref[...] * DK ** (-0.5), k_ref[...]
    grow, shrink = jnp.exp(run - middle), jnp.exp(middle - run)
    from_start, to_end = jnp.exp(run), jnp.exp(closing - run)
    near_q, near_k = halves(q * grow), halves(k * shrink)
    v, dout = halves(v_ref[...]), halves(dmixed_ref[...])
    after_parts = halves(after)
    keep = triangle(True)
    scores = halves(jnp.where(keep, fine(near_q, near_k, NT), 0.0))
    dscores = halves(jnp.where(keep, fine(dout, v, NT), 0.0))
    tail = k * to_end
    dtail = fine(v, after_parts, NT)
    dq = fine(dscores, near_k) * grow + fine(dout, halves(begin), NT) * from_start
    dk = fine(dscores, near_q, TN) * shrink + dtail * to_end
    dv = fine(scores, dout, TN) + fine(halves(tail), after_parts)
    ones = jnp.ones((16, DV), LOW)
    high, low = halves(begin * after)
    across = (dot(ones, high, NT) + dot(ones, low, NT))[0:1, :]
    dclosing = jnp.sum(dtail * tail, axis=0, keepdims=True) + jnp.exp(closing) * across
    ddecay = running_sum(dq * q - dk * k, lower=False) + dclosing
    dlogits = ddecay * jax.nn.sigmoid(-logits_ref[...]) * (1.0 / 16.0)
    dlogits_ref[...] = dlogits
    dbias_ref[...] += jnp.sum(dlogits, axis=0, keepdims=True)
    back_ref[:, :DV] = dv.astype(LOW)
    back_ref[:, DV : DV + DK] = dk.astype(LOW)
    back_ref[:, DV + DK :] = (dq * DK ** (-0.5)).astype(LOW)
    before = widen(jnp.exp(column_sum(decay)), DV) * after + fine(halves(q * from_start), dout, TN)
    state[...] = jnp.where(info[1 + at] > 0, jnp.zeros_like(before), before)


PARAMS = pltpu.CompilerParams(
    dimension_semantics=("arbitrary",), vmem_limit_bytes=40 * 1024 * 1024
)
QUICK = pl.CostEstimate(flops=1, bytes_accessed=1, transcendentals=0)


def token_call(kernel, info, count, quarter, reverse, inputs, outputs, scratch):
    per = quarter // BLOCK

    def place(i):
        return count - 1 - i if reverse else i

    def spec(shape, column):
        if column is None:
            return pl.BlockSpec(shape, lambda i, info: (0, 0))
        if column == "state":
            return pl.BlockSpec(shape, lambda i, info: (place(i), 0, 0))

        def index(i, info):
            j = place(i)
            return ((j // per) ^ info[0]) * per + j % per, column

        return pl.BlockSpec(shape, index)

    return pl.pallas_call(
        kernel,
        grid_spec=pltpu.PrefetchScalarGridSpec(
            num_scalar_prefetch=1,
            grid=(count,),
            in_specs=[spec(shape, column) for _, shape, column in inputs],
            out_specs=[spec(shape, column) for _, shape, column in outputs],
            scratch_shapes=scratch,
        ),
        out_shape=[out for out, _, _ in outputs],
        compiler_params=PARAMS,
        cost_estimate=QUICK,
    )(info, *[array for array, _, _ in inputs])


def shape_of(*extent, dtype=FULL):
    return jax.ShapeDtypeStruct(extent, dtype)


def fill(piece_refs, places, weight_refs, spans):
    for (piece, source, target, size), (start, stop), weight in (
        (place, span, weight) for place in places for span, weight in zip(spans, weight_refs)
    ):
        weight[target : target + size, :] = piece_refs[piece][source : source + size, start:stop]


def assemble_kernel(places, spans, dotted, x_ref, *refs):
    number = 1 + max(p[0] for p in places)
    pieces, y_ref, weights = refs[:number], refs[number], refs[number + 1 :]

    @pl.when(pl.program_id(0) == 0)
    def _():
        fill(pieces, places, weights, spans)

    for i in range(dotted):
        start, stop = spans[i]
        y_ref[:, start:stop] = dot(x_ref[...], weights[i][...])


def assemble_back_kernel(places, x_ref, pre_ref, *refs):
    number = 1 + max(p[0] for p in places)
    pieces, back_ref, weight = refs[:number], refs[number], refs[number + 1]
    ff = weight.shape[1]

    @pl.when(pl.program_id(0) == 0)
    def _():
        fill(pieces, places, [weight], [(0, ff)])

    grad = dot(x_ref[...], weight[...])
    pre, up = pre_ref[:, :ff], pre_ref[:, ff:]
    soft = jax.nn.sigmoid(pre)
    back_ref[:, :ff] = (grad * up * (soft * (1.0 + pre * (1.0 - soft)))).astype(LOW)
    back_ref[:, ff:] = (grad * (pre * soft)).astype(LOW)


def assemble_gate_kernel(places, x_ref, *refs):
    number = 1 + max(p[0] for p in places)
    pieces, pre_ref, weight, inner_ref = refs[:number], *refs[number:]
    ff = weight.shape[1] // 2

    @pl.when(pl.program_id(0) == 0)
    def _():
        fill(pieces, places, [weight], [(0, 2 * ff)])

    pre_ref[...] = dot(x_ref[...], weight[...])
    gate = pre_ref[:, :ff]
    inner_ref[...] = (gate * jax.nn.sigmoid(gate) * pre_ref[:, ff:]).astype(LOW)


def product_kernel(number, *refs):
    kept_ref, sent_ref = refs[2 * number :]
    total = 0.0
    for x_ref, w_ref in zip(refs[:number], refs[number : 2 * number]):
        total = total + dot(x_ref[...], w_ref[...], NT)
    half = kept_ref.shape[0]
    kept_ref[...] = total[:half]
    sent_ref[...] = total[half:].astype(LOW)


def product_call(pairs, block, half):
    tile = 512
    width = pairs[0][1].shape[0]
    out = pl.BlockSpec((half, tile), lambda i: (0, i))
    return pl.pallas_call(
        functools.partial(product_kernel, len(pairs)),
        grid=(width // tile,),
        in_specs=[
            pl.BlockSpec((2 * half, x.shape[1]), lambda i: (block, 0), pipeline_mode=pl.Buffered(1))
            for x, _ in pairs
        ]
        + [pl.BlockSpec((tile, w.shape[1]), lambda i: (i, 0)) for _, w in pairs],
        out_specs=[out, out],
        out_shape=[shape_of(half, width), shape_of(half, width, dtype=LOW)],
        compiler_params=PARAMS,
        cost_estimate=QUICK,
    )(*[x for x, _ in pairs], *[w for _, w in pairs])


def parts_kernel(number, targets, wide, table, *refs):
    outs = refs[2 * number :]
    values = [dot(l[...], r[...], TN) for l, r in zip(refs[:number], refs[number : 2 * number])]
    for step, (target, row) in enumerate(targets):

        @pl.when(pl.program_id(0) == step)
        def _():
            start = 0
            for value in values:
                stop = start + value.shape[1]
                outs[target][row * wide : (row + 1) * wide, start:stop] = value.astype(outs[target].dtype)
                start = stop


def parts_call(pairs, groups, wide, dtype):
    columns = sum(r.shape[1] for _, r in pairs)
    if wide % LANES:
        def part(k):
            cut = slice(k * wide, (k + 1) * wide)
            return jnp.concatenate([dot(l[:, cut], r, TN) for l, r in pairs], axis=1)

        return [jnp.concatenate([part(k) for k in group], axis=0).astype(dtype) for group in groups]
    flat = [(j, i, k) for j, group in enumerate(groups) for i, k in enumerate(group)]

    def fixed(shape):
        return pl.BlockSpec(shape, lambda i, table: (0, 0), pipeline_mode=pl.Buffered(1))

    return pl.pallas_call(
        functools.partial(parts_kernel, len(pairs), [(j, i) for j, i, _ in flat], wide),
        grid_spec=pltpu.PrefetchScalarGridSpec(
            num_scalar_prefetch=1,
            grid=(len(flat),),
            in_specs=[pl.BlockSpec((l.shape[0], wide), lambda i, table: (0, table[i])) for l, _ in pairs]
            + [fixed(r.shape) for _, r in pairs],
            out_specs=[fixed((len(g) * wide, columns)) for g in groups],
        ),
        out_shape=[shape_of(len(g) * wide, columns, dtype=dtype) for g in groups],
        compiler_params=PARAMS,
        cost_estimate=QUICK,
    )(jnp.asarray([k for _, _, k in flat], jnp.int32), *[l for l, _ in pairs], *[r for _, r in pairs])


def once(shape):
    return pl.BlockSpec(shape, lambda i: (0, 0), pipeline_mode=pl.Buffered(1))


def assemble_call(kernel, x, extra, pieces, out_width, out_dtype, spans, depth, also=None):
    tile = 256
    rows = lambda width: pl.BlockSpec((tile, width), lambda i: (i, 0))
    return pl.pallas_call(
        kernel,
        grid=(x.shape[0] // tile,),
        in_specs=[rows(x.shape[1])]
        + [rows(e.shape[1]) for e in extra]
        + [once(p.shape) for p in pieces],
        out_specs=[rows(out_width)]
        + [once((depth, stop - start)) for start, stop in spans]
        + ([rows(also)] if also else []),
        out_shape=[shape_of(x.shape[0], out_width, dtype=out_dtype)]
        + [shape_of(depth, stop - start, dtype=LOW) for start, stop in spans]
        + ([shape_of(x.shape[0], also, dtype=LOW)] if also else []),
        compiler_params=pltpu.CompilerParams(
            dimension_semantics=("arbitrary",), vmem_limit_bytes=52 * 1024 * 1024
        ),
        cost_estimate=QUICK,
    )(x, *extra, *pieces)


def columns_in_kernel(order, core, a, b, c, d, oa, ob, oc, od):
    oa[...] = a[...]
    ob[...] = b[...]
    oc[...] = c[...]
    od[...] = d[...]


def columns_in(hidden, cotangent, gain_a, gain_b, order, core, quarter, wide):
    count = order.shape[0]
    if wide % LANES:
        def pick(x):
            return jnp.concatenate(
                [lax.dynamic_slice_in_dim(x, order[i] * wide, wide, 1) for i in range(count)], axis=1
            )

        def rows(x):
            return lax.dynamic_slice_in_dim(x, core * quarter, quarter, 0)

        return pick(rows(hidden)), pick(rows(cotangent)), pick(gain_a), pick(gain_b)
    big = pl.BlockSpec((quarter, wide), lambda i, order, core: (core[0], order[i]))
    small = pl.BlockSpec((1, wide), lambda i, order, core: (0, order[i]))
    big_out = pl.BlockSpec((quarter, wide), lambda i, order, core: (0, i))
    small_out = pl.BlockSpec((1, wide), lambda i, order, core: (0, i))
    total = count * wide
    return pl.pallas_call(
        columns_in_kernel,
        grid_spec=pltpu.PrefetchScalarGridSpec(
            num_scalar_prefetch=2,
            grid=(count,),
            in_specs=[big, big, small, small],
            out_specs=[big_out, big_out, small_out, small_out],
        ),
        out_shape=[
            shape_of(quarter, total, dtype=LOW),
            shape_of(quarter, total, dtype=LOW),
            shape_of(1, total),
            shape_of(1, total),
        ],
        compiler_params=PARAMS,
    )(order, core.reshape(1), hidden, cotangent, gain_a, gain_b)


def columns_out_kernel(order, core, mine, near, out):
    quarter = mine.shape[0]
    first = core[0] == 0
    out[:quarter, :] = jnp.where(first, mine[...], near[...])
    out[quarter:, :] = jnp.where(first, near[...], mine[...])


def columns_out(mine, near, order, inverse, core, wide):
    quarter, total = mine.shape
    count = order.shape[0]
    if wide % LANES:
        first = core == 0
        both = jnp.concatenate([jnp.where(first, mine, near), jnp.where(first, near, mine)], axis=0)
        return jnp.concatenate(
            [lax.dynamic_slice_in_dim(both, inverse[i] * wide, wide, 1) for i in range(count)], axis=1
        )
    spec = pl.BlockSpec((quarter, wide), lambda i, order, core: (0, i))
    return pl.pallas_call(
        columns_out_kernel,
        grid_spec=pltpu.PrefetchScalarGridSpec(
            num_scalar_prefetch=2,
            grid=(count,),
            in_specs=[spec, spec],
            out_specs=pl.BlockSpec((2 * quarter, wide), lambda i, order, core: (0, order[i])),
        ),
        out_shape=shape_of(2 * quarter, total, dtype=mine.dtype),
        compiler_params=PARAMS,
    )(order, core.reshape(1), mine, near)


def block_resets(lengths, dealing, count, start):
    number = lengths.shape[0]
    picks = (dealing[:, None] == jnp.arange(number, dtype=jnp.int32)[None, :]).astype(jnp.int32)
    placed = jnp.sum(picks * lengths[None, :], axis=1, dtype=jnp.int32)
    ends = jnp.cumsum(placed, dtype=jnp.int32)
    starts = ends - placed
    firsts = start + jnp.arange(count, dtype=jnp.int32)
    return jnp.any(firsts[:, None] == starts[None, :], axis=1).astype(jnp.int32)


def tied(*values):
    return lax.optimization_barrier(values)


def silu(x):
    return x * jax.nn.sigmoid(x)


def shards(
    hidden_in,
    cotangent,
    lengths,
    dealing,
    norm_attn,
    w_query,
    w_key,
    w_value,
    w_rank_in,
    w_rank_out,
    decay_bias,
    w_gate_out,
    head_gain,
    w_out,
    norm_mlp,
    w_ff_gate,
    w_ff_up,
    w_ff_down,
):
    peers = lax.axis_size("seq")
    place, core = lax.axis_index("seq"), lax.axis_index("head")
    laps, groups = peers // 4, peers // 2
    group, left = place // 2, place % 2 == 0
    rows, width = hidden_in.shape
    quarter = rows // 2
    tokens = 4 * quarter
    count = tokens // BLOCK
    wide = width // groups
    ff = w_ff_gate.shape[1] // 2

    def pair(x):
        return lax.ppermute(x, "seq", [(i, i ^ 1) for i in range(peers)])

    def side(x):
        return lax.ppermute(x, "seq", [(i, i ^ 2) for i in range(peers)])

    def ring(x):
        return lax.ppermute(x, "seq", [(i, (i + 4) % peers) for i in range(peers)])

    def twin(x):
        return lax.ppermute(x, "head", [(0, 1), (1, 0)])

    lap, flank = group // 2, group % 2
    steps = jnp.arange(groups, dtype=jnp.int32)
    order = ((lap - steps % laps) % laps) * 2 + (flank ^ (steps // laps))
    inverse = (flank ^ (steps % 2)) * laps + (lap - steps // 2) % laps
    resets = block_resets(lengths, dealing, count, group * count)
    ahead = jnp.cumsum(resets)
    info = jnp.concatenate(
        [
            ((place % 2) * 2 + core).astype(jnp.int32).reshape(1),
            resets,
            (ahead == ahead[-1]).astype(jnp.int32),
            (ahead == 0).astype(jnp.int32),
            (ahead[-1:] == 0).astype(jnp.int32),
        ]
    )

    def split(*arrays):
        mid = [a.shape[1] // 2 for a in arrays]
        low = jnp.concatenate([a[:, :m] for a, m in zip(arrays, mid)], axis=1)
        high = jnp.concatenate([a[:, m:] for a, m in zip(arrays, mid)], axis=1)
        return jnp.where(left, low, high), jnp.where(left, high, low)

    def turned_over(x):
        return with_layout_constraint(x.T, Layout((0, 1)))

    def joined(mine, got):
        return jnp.concatenate(
            [jnp.where(left, mine, got), jnp.where(left, got, mine)], axis=0
        )

    class Gather:
        def __init__(self, own):
            self.blocks, self.others = [own], []

        def ring(self):
            if len(self.blocks) < laps:
                self.blocks.append(ring(self.blocks[-1]))

        def side(self, number=1):
            for _ in range(number):
                if len(self.others) < min(laps, len(self.blocks)):
                    self.others.append(side(self.blocks[len(self.others)]))

        def rest(self):
            while len(self.blocks) < laps:
                self.ring()

        def pieces(self):
            arrays = self.blocks + self.others
            return arrays, [(i, 0, i * wide, wide) for i in range(len(arrays))]

    class GatherSide(Gather):
        def begin(self):
            self.got = side(self.blocks[0])

        def join(self):
            self.blocks = [jnp.concatenate([self.blocks[0], self.got], axis=0)]

        def pieces(self):
            places = [(i, 0, i * wide, wide) for i in range(laps)]
            places += [(i, wide, (laps + i) * wide, wide) for i in range(laps)]
            return self.blocks, places

    class Reduce:
        def __init__(self, *pairs):
            self.pairs = pairs
            self.turn = [(p + 1) % laps for p in range(laps)]
            self.parts, self.owns, self.sent, self.flown = [], [], [], None
            self.done = 0

        def make(self):
            self.parts = list(parts_call(self.pairs, [[laps + p] for p in self.turn], wide, LOW))

        def make_own(self):
            self.owns = list(parts_call(self.pairs, [[p] for p in self.turn], wide, FULL))

        def send(self, number=1):
            for _ in range(number):
                if len(self.sent) < laps:
                    self.sent.append(side(self.parts[len(self.sent)]))

        def add(self):
            while len(self.sent) <= self.done:
                self.send()
            value = self.owns[self.done] + self.sent[self.done]
            if self.flown is not None:
                value = value + self.flown
            self.done += 1
            return value

        def hop(self):
            if self.done < laps - 1:
                self.flown = ring(self.add().astype(LOW))

        def last(self):
            while self.done < laps - 1:
                self.hop()
            self.total = self.add()

        def halve(self):
            total = self.total
            top, low = total[: wide // 2], total[wide // 2 :]
            self.mine = jnp.where(left, top, low)
            self.got = pair(jnp.where(left, low, top).astype(LOW))

        def out(self):
            got = self.got.astype(FULL)
            return jnp.where(left, self.mine, got), jnp.where(left, got, self.mine)

    class ReduceSide(Reduce):
        def make(self):
            p = self.turn[0]
            (self.value,) = parts_call(self.pairs, [[p, laps + p]], wide, LOW)

        def make_own(self):
            self.owns = [None] + list(
                parts_call(self.pairs, [[p, laps + p] for p in self.turn[1:]], wide, FULL)
            )

        def fly(self):
            self.done = 1
            self.flown = ring(self.value)

        def add(self):
            value = self.owns[self.done] + self.flown
            self.done += 1
            return value

        def cross(self):
            while self.done < laps - 1:
                self.hop()
            total = self.add()
            self.kept = total[:wide]
            self.come = side(total[wide:].astype(LOW))

        def last(self):
            self.total = self.kept + self.come

    def together(*things):
        def read(holder, key):
            return holder[key] if isinstance(key, int) else getattr(holder, key)

        values = [read(*t) if isinstance(t, tuple) else t for t in things]
        values = lax.optimization_barrier(values)
        back = []
        for thing, value in zip(things, values):
            if not isinstance(thing, tuple):
                back.append(value)
            elif isinstance(thing[1], int):
                thing[0][thing[1]] = value
            else:
                setattr(*thing, value)
        return back[0] if len(back) == 1 else back

    def spread_near(x):
        return pair(x), twin(x)

    def spread_all(x, far, near, other):
        return jnp.concatenate([x, near, far, other], axis=0)

    q2 = 2 * quarter

    def far_part(*pairs):
        return list(product_call(pairs, 1, quarter))

    def near_part(*pairs):
        return list(product_call(pairs, 0, quarter))

    def summed_pair(kept, sent):
        return kept + twin(sent)

    mine, other = split(w_value, w_key)
    got = pair(other)
    hidden_low, cot_own, gain_attn, gain_mlp = columns_in(
        hidden_in, cotangent, norm_attn[None], norm_mlp[None], order, core, quarter, wide
    )
    hidden = hidden_low.astype(FULL)
    scale_attn = lax.rsqrt(jnp.mean(hidden * hidden, axis=1, keepdims=True) + EPSILON)
    first_own = (hidden * scale_attn * gain_attn).astype(LOW)
    got, first_own, cot_own, w_rank_in, w_gate_out, w_query, w_out = together(
        got, first_own, cot_own, w_rank_in, w_gate_out, w_query, w_out
    )
    keys = Gather(joined(mine, got))
    keys.ring()
    keys.side()
    far, near = spread_near(first_own)
    mine, other = split(w_gate_out, w_query, turned_over(w_out))
    mine, other, w_ff_gate, w_ff_up, w_ff_down, w_rank_in = together(
        mine, other, (keys.blocks, 1), w_ff_gate, w_ff_up, w_ff_down, w_rank_in
    )
    keys.ring()
    keys.side()
    got = pair(other)
    mine_b, other_b = split(w_ff_gate, w_ff_up, turned_over(w_ff_down))
    rank_weight = jnp.concatenate(
        [lax.dynamic_slice_in_dim(w_rank_in, order[i] * wide, wide, 0) for i in range(groups)], axis=0
    )
    far, near, mine_b, other_b, rank_weight = together(
        (keys.blocks, 2), (keys.others, 0), far, near, mine_b, other_b, rank_weight
    )
    keys.rest()
    keys.side()
    other = twin(far)
    got_b = pair(other_b)
    first = spread_all(first_own, far, near, other)
    first, got = together((keys.blocks, laps - 1), (keys.others, 1), first, got)
    keys.side(laps)
    gates = Gather(joined(mine, got))
    gates.ring()
    rank_in = dot(first, rank_weight).astype(LOW)
    rank_out = jnp.where(left, w_rank_out[:, :DK], w_rank_out[:, DK:])
    bias = jnp.where(left, decay_bias[:DK], decay_bias[DK:])
    logits = dot(rank_in, rank_out) + bias
    decay = jax.nn.log_sigmoid(logits) / 16.0
    first, rank_in, decay, logits = together(
        *[(keys.others, i) for i in range(2, laps)],
        (gates.blocks, 0),
        (gates.blocks, 1),
        first,
        rank_in,
        decay,
        logits,

    )
    gates.ring()
    gates.side()
    arrays, places = keys.pieces()
    span = [(0, DV + DK)]
    keyed, full_k = assemble_call(
        functools.partial(assemble_kernel, places, span, 1), first, [], arrays, DV + DK, FULL, span, width
    )
    gain = head_gain[None]
    state_scratch = pltpu.VMEM((DK, DV), FULL)
    row_scratch = pltpu.VMEM((8, DK), FULL)
    key_block, val_block = (BLOCK, DK), (BLOCK, DV)
    state_shape = (DK, DV)
    call = functools.partial(token_call, info=info, count=count, quarter=quarter)
    (summary,) = call(
        summary_kernel,
        reverse=True,
        inputs=[(keyed, key_block, 2), (keyed, val_block, 0), (decay, key_block, 0)],
        outputs=[(shape_of(DK, DV + LANES, dtype=LOW), (DK, DV + LANES), None)],
        scratch=[state_scratch, row_scratch, pltpu.VMEM((DK, LANES), FULL)],
    )
    summary, got_b = together((gates.blocks, 2), (gates.others, 0), summary, got_b)
    gates.rest()
    gates.side()
    halves_of_seq = [[i for i in range(peers) if i % 2 == k] for k in range(2)]
    slab = DK // groups

    def turned(x):
        return lax.all_to_all(x, "seq", 0, 0, axis_index_groups=halves_of_seq, tiled=True)

    pieces = turned(summary).reshape(groups, slab, DV + LANES)
    pair_b = joined(mine_b, got_b)
    ffs = Gather(pair_b[:, : 2 * ff])
    downs = GatherSide(pair_b[:, 2 * ff :])
    downs.begin()
    cot_far, cot_near = spread_near(cot_own)
    pieces, ffs.blocks[0], cot_far, cot_near = together(
        (gates.blocks, laps - 1),
        (gates.others, 1),
        (downs, "got"),
        pieces,
        ffs.blocks[0],
        cot_far,
        cot_near,
    )
    gates.side(laps)
    downs.join()
    ffs.ring()
    cot_other = twin(cot_far)
    entering = turned(chain_call(pieces, pieces, False).reshape(DK, DV))
    entering, keyed, first, cot_other, downs.blocks[0] = together(
        *[(gates.others, i) for i in range(2, laps)],
        (ffs.blocks, 1),
        entering,
        keyed,
        first,
        cot_other,
        downs.blocks[0],
    )
    ffs.ring()
    ffs.side()
    cot = spread_all(cot_own, cot_far, cot_near, cot_other)
    arrays, places = gates.pieces()
    span = [(0, DV), (DV, DV + DK), (DV + DK, 2 * DV + DK)]
    gated_in, full_g, full_q, full_o = assemble_call(
        functools.partial(assemble_kernel, places, span, 2), first, [], arrays, DV + DK, FULL, span, width
    )
    mixed, gated, states = call(
        mix_kernel,
        reverse=False,
        inputs=[
            (gated_in, key_block, 2),
            (keyed, key_block, 2),
            (keyed, val_block, 0),
            (gated_in, val_block, 0),
            (decay, key_block, 0),
            (entering, state_shape, None),
            (gain, (1, DV), None),
        ],
        outputs=[
            (shape_of(tokens, DV), val_block, 0),
            (shape_of(tokens, DV, dtype=LOW), val_block, 0),
            (shape_of(count, DK, DV), (1, DK, DV), "state"),
        ],
        scratch=[state_scratch],
    )

    gated, cot = together((ffs.blocks, 2), (ffs.others, 0), gated, cot)
    far, gated = together(summed_pair(*far_part((gated, full_o))).astype(LOW), gated)
    ffs.rest()
    ffs.side()
    got = pair(far)
    near = near_part((gated, full_o))
    got, near = together((ffs.blocks, laps - 1), (ffs.others, 1), got, near)
    resid = hidden + (summed_pair(*near) + got)
    scale_mlp = lax.rsqrt(jnp.mean(resid * resid, axis=1, keepdims=True) + EPSILON)
    second_own = together((resid * scale_mlp * gain_mlp).astype(LOW))
    ffs.side()
    downs.ring()
    far, near = spread_near(second_own)
    far, near, second_own = together(
        (ffs.others, 2), (downs.blocks, 1), far, near, second_own
    )
    ffs.side(laps)
    downs.ring()
    other = twin(far)
    second = spread_all(second_own, far, near, other)
    second, cot = together(*[(ffs.others, i) for i in range(3, laps)], (downs.blocks, 2), second, cot)
    downs.rest()
    arrays, places = ffs.pieces()
    span = [(0, 2 * ff)]
    ff_both, full_f, inner = assemble_call(
        functools.partial(assemble_gate_kernel, places), second, [], arrays, 2 * ff, FULL, span, width, ff
    )
    down_grad = ReduceSide((cot, inner))
    down_grad.make()
    inner, ff_both, cot, second = together(
        (downs.blocks, laps - 1), (down_grad, "value"), inner, ff_both, cot, second
    )
    down_grad.fly()
    down_grad.pairs = ((cot, inner),)
    arrays, places = downs.pieces()
    both_back, full_d = assemble_call(
        functools.partial(assemble_back_kernel, places), cot, [ff_both], arrays, 2 * ff, LOW, [(0, ff)], width
    )

    gate_grad = Reduce((second, both_back[:, :ff]))
    gate_grad.make()
    far = far_part((both_back, full_f))
    far, both_back, second, full_d, full_f, inner, cot = together(
        (down_grad, "flown"), (gate_grad, "parts"), far, both_back, second, full_d, full_f, inner, cot
    )
    far, both_back, second, full_f, inner, cot, down_grad.flown = together(
        summed_pair(*far).astype(LOW), both_back, second, full_f, inner, cot, down_grad.flown
    )
    down_grad.pairs = ((cot, inner),)
    gate_grad.pairs = ((second, both_back[:, :ff]),)
    got = pair(far)
    gate_grad.send(2)
    down_grad.make_own()
    down_grad.hop()
    near = near_part((both_back, full_f))
    up_grad = Reduce((second, both_back[:, ff:]))
    up_grad.make()
    got, near, both_back, second = together(
        (down_grad, "flown"),
        (down_grad, "owns"),
        (up_grad, "parts"),
        (gate_grad.sent, 0),
        (gate_grad.sent, 1),
        got,
        near,
        both_back,
        second,
    )
    gate_grad.pairs = ((second, both_back[:, :ff]),)
    up_grad.pairs = ((second, both_back[:, ff:]),)

    def norm_back(grad, value, scale, gains):
        normed = value * scale
        scaled = grad * gains
        gain_grad = jnp.sum(grad * normed, axis=0, keepdims=True)
        return scale * (scaled - normed * jnp.mean(scaled * normed, axis=1, keepdims=True)), gain_grad

    resid_norm, grad_gain_mlp = norm_back(summed_pair(*near) + got, resid, scale_mlp, gain_mlp)
    grad_resid = cot_own.astype(FULL) + resid_norm
    back_own, both_back, second, down_grad.owns, down_grad.flown = together(
        grad_resid.astype(LOW), both_back, second, down_grad.owns, down_grad.flown
    )
    gate_grad.pairs = ((second, both_back[:, :ff]),)
    up_grad.pairs = ((second, both_back[:, ff:]),)
    far, near = spread_near(back_own)
    gate_grad.send(laps)
    down_grad.hop()
    gate_grad.make_own()
    up_grad.make_own()
    far, near, back_own = together(
        (gate_grad, "owns"), (up_grad, "owns"), (gate_grad.sent, 2), far, near, back_own
    )
    other = twin(far)
    resid_back, full_d, inner, full_o, gate_grad.sent[0] = together(
        spread_all(back_own, far, near, other), full_d, inner, full_o, gate_grad.sent[0]
    )
    up_grad.send()
    gate_grad.hop()
    grad_gated = dot(resid_back, full_o)
    gate_back, dmixed, summary_back, grad_gain_head = call(
        gate_back_kernel,
        reverse=False,
        inputs=[
            (gated_in, key_block, 2),
            (gated_in, val_block, 0),
            (decay, key_block, 0),
            (mixed, val_block, 0),
            (grad_gated, val_block, 0),
            (gain, (1, DV), None),
        ],
        outputs=[
            (shape_of(tokens, DV, dtype=LOW), val_block, 0),
            (shape_of(tokens, DV), val_block, 0),
            (shape_of(DK, DV, dtype=LOW), state_shape, None),
            (shape_of(1, DV), (1, DV), None),
        ],
        scratch=[state_scratch, row_scratch],
    )
    summary_back, resid_back, gate_back, first, gated = together(
        (up_grad.sent, 0),
        (down_grad, "flown"),
        *[(gate_grad.sent, i) for i in range(3, laps)],
        (gate_grad, "flown"),
        summary_back,
        resid_back,
        gate_back,
        first,
        gated,
    )
    up_grad.send()
    gate_grad.hop()
    pieces_back = turned(summary_back).reshape(groups, slab, DV)
    out_grad = Reduce((resid_back, gated), (first, gate_back))
    out_grad.make()
    pieces_back, full_d, inner, resid_back, gate_back, first, gated = together(
        (up_grad.sent, 1),
        (gate_grad, "flown"),
        (out_grad, "parts"),
        pieces_back,
        full_d,
        inner,
        resid_back,
        gate_back,
        first,
        gated,
    )
    leaving, gate_grad.flown, up_grad.sent[0] = together(
        chain_call(pieces, pieces_back, True), gate_grad.flown, up_grad.sent[0]
    )
    out_grad.pairs = ((resid_back, gated), (first, gate_back))
    up_grad.send(laps)
    gate_grad.hop()
    up_grad.hop()
    leaving = turned(leaving.reshape(DK, DV))
    out_far, out_near = far_part((inner, full_d)), near_part((inner, full_d))
    leaving, keyed, out_far, out_near = together(
        (gate_grad, "flown"),
        (up_grad, "flown"),
        *[(up_grad.sent, i) for i in range(2, laps)],
        leaving,
        keyed,
        out_far,
        out_near,
    )
    down_grad.cross()
    out_grad.send()
    up_grad.hop()
    mixes_back, grad_logits, grad_bias = call(
        mix_back_kernel,
        reverse=True,
        inputs=[
            (gated_in, key_block, 2),
            (keyed, key_block, 2),
            (keyed, val_block, 0),
            (decay, key_block, 0),
            (logits, key_block, 0),
            (states, (1, DK, DV), "state"),
            (dmixed, val_block, 0),
            (leaving, state_shape, None),
        ],
        outputs=[
            (shape_of(tokens, DV + 2 * DK, dtype=LOW), (BLOCK, DV + 2 * DK), 0),
            (shape_of(tokens, DK), key_block, 0),
            (shape_of(1, DK), (1, DK), None),
        ],
        scratch=[state_scratch],
    )
    mixes_back, grad_logits, first, resid_back, gate_back, full_k, full_q, full_g = together(
        (up_grad, "flown"),
        (out_grad.sent, 0),
        (down_grad, "come"),
        mixes_back,
        grad_logits,
        first,
        resid_back,
        gate_back,
        full_k,
        full_q,
        full_g,
    )
    out_grad.pairs = ((resid_back, gated), (first, gate_back))
    out_grad.send(2)
    mix_grad = Reduce((first, mixes_back))
    mix_grad.make()
    full_vkq = jnp.concatenate([full_k, full_q], axis=1)
    precise = lax.Precision.HIGHEST
    grad_rank = lax.dot_general(
        grad_logits, rank_out.astype(FULL), (NT, ((), ())), precision=precise
    )
    rank_high = grad_rank.astype(LOW)
    rank_low = (grad_rank - rank_high.astype(FULL)).astype(LOW)

    back_pairs = (
        (mixes_back, full_vkq),
        (gate_back, full_g),
        (rank_high, rank_weight),
        (rank_low, rank_weight),
    )
    far = far_part(*back_pairs)
    far, first, back_pairs, resid_back, gate_back, gated = together(
        (out_grad.sent, 1), (mix_grad, "parts"), far, first, list(back_pairs), resid_back, gate_back, gated
    )
    far, first, back_pairs, resid_back, gate_back, gated, grad_logits, up_grad.flown = together(
        summed_pair(*far).astype(LOW), first, back_pairs, resid_back, gate_back, gated, grad_logits, up_grad.flown
    )
    mixes_back, rank_high, rank_low = back_pairs[0][0], back_pairs[2][0], back_pairs[3][0]
    mix_grad.pairs = ((first, mixes_back),)
    out_grad.pairs = ((resid_back, gated), (first, gate_back))
    got = pair(far)
    out_grad.send(laps)
    mix_grad.send()
    out_grad.make_own()
    out_grad.hop()
    up_grad.hop()
    near = near_part(*back_pairs)
    mix_grad.make_own()
    grad_rank_in = dot(rank_high, first, TN) + dot(rank_low, first, TN)
    grad_rank_out = lax.dot_general(
        rank_in.astype(FULL), grad_logits, (TN, ((), ())), precision=precise
    )
    got, near, grad_rank_in, grad_rank_out, out_far, out_near = together(
        *[(out_grad.sent, i) for i in range(2, laps)],
        (mix_grad.sent, 0),
        (mix_grad, "owns"),
        (out_grad, "flown"),
        (up_grad, "flown"),
        got,
        near,
        grad_rank_in,
        grad_rank_out,
        summed_pair(*out_far).astype(LOW),
        summed_pair(*out_near),
    )
    mix_grad.send()
    mix_grad.hop()
    out_grad.hop()
    out_got = pair(out_far)
    hidden_norm, grad_gain_attn = norm_back(summed_pair(*near) + got, hidden, scale_attn, gain_attn)
    input_own = grad_resid + hidden_norm
    input_own, grad_gain_attn = together(
        (mix_grad.sent, 1), (mix_grad, "flown"), (out_grad, "flown"), input_own, grad_gain_attn
    )
    mix_grad.send()
    mix_grad.hop()
    down_grad.last()
    down_grad.halve()
    input_near = twin(input_own)

    def unordered(x):
        return jnp.concatenate(
            [lax.dynamic_slice_in_dim(x, inverse[i] * wide, wide, 1) for i in range(groups)], axis=1
        )

    wide_part = jnp.concatenate(
        [grad_rank_in, grad_gain_attn, grad_gain_mlp, jnp.zeros((6, width), FULL)], axis=0
    )
    wide_part = unordered(wide_part + twin(wide_part))
    empty = jnp.zeros_like(grad_rank_out)
    rank_part = jnp.concatenate(
        [jnp.where(left, grad_rank_out, empty), jnp.where(left, empty, grad_rank_out)], axis=1
    )
    bias_part = jnp.concatenate(
        [jnp.where(left, grad_bias, 0.0), jnp.where(left, 0.0, grad_bias)], axis=1
    )
    head_part = grad_gain_head + twin(grad_gain_head)
    narrow_part = jnp.concatenate(
        [rank_part, bias_part, head_part, jnp.zeros((6, 2 * DK), FULL)], axis=0
    )
    small = jnp.concatenate([wide_part, narrow_part], axis=1)
    input_near, small, out_got = together(
        (mix_grad.sent, 2), (mix_grad, "flown"), (down_grad, "got"), input_near, small, out_got
    )
    hops = [1 << k for k in (0, *range(2, peers.bit_length() - 1), 1)]

    def summed(small):
        hop = hops.pop(0)
        return small + lax.ppermute(small, "seq", [(i, i ^ hop) for i in range(peers)])

    mix_grad.send(laps)
    mix_grad.hop()
    out_grad.hop()
    small = summed(small)
    gate_grad.last()
    gate_grad.halve()
    grad_input = columns_out(input_own, input_near, order, inverse, core, wide)
    small, grad_input = together(
        *[(mix_grad.sent, i) for i in range(3, laps)],
        (mix_grad, "flown"),
        (out_grad, "flown"),
        (gate_grad, "got"),
        small,
        grad_input,
    )
    mix_grad.last()
    mix_grad.halve()
    small = summed(small)
    small = together((mix_grad, "got"), small)
    small = summed(small)
    up_grad.last()
    up_grad.halve()
    small = together((up_grad, "got"), small)
    out_grad.last()
    out_grad.halve()
    out_own = (resid + (out_near + out_got)).astype(LOW)
    block_out = columns_out(out_own, twin(out_own), order, inverse, core, wide)
    while hops:
        small = summed(small)
    down_halves, gate_halves, up_halves = down_grad.out(), gate_grad.out(), up_grad.out()
    out_halves, mix_halves = out_grad.out(), mix_grad.out()

    def beside(pieces, start, stop):
        return jnp.concatenate([half[:, start:stop] for half in pieces], axis=1)

    return (
        block_out,
        grad_input,
        small[16, :width],
        beside(mix_halves, DV + DK, DV + 2 * DK),
        beside(mix_halves, DV, DV + DK),
        beside(mix_halves, 0, DV),
        small[:16, :width].T,
        small[:16, width:],
        small[16, width:],
        beside(out_halves, DV, 2 * DV),
        small[17, width:],
        beside(out_halves, 0, DV).T,
        small[17, :width],
        jnp.concatenate(gate_halves, axis=1),
        jnp.concatenate(up_halves, axis=1),
        jnp.concatenate(down_halves, axis=1).T,
    )


def solution(mesh):
    return jax.shard_map(
        shards,
        mesh=mesh,
        in_specs=(
            P("seq", None),
            P("seq", None),
            P(),
            P(),
            P(),
            P("seq", "head"),
            P("seq", "head"),
            P("seq", "head"),
            P(),
            P(None, "head"),
            P("head"),
            P("seq", "head"),
            P(),
            P("head", "seq"),
            P(),
            P("seq", "head"),
            P("seq", "head"),
            P("head", "seq"),
        ),
        out_specs=(
            P("seq", None),
            P("seq", None),
            P(),
            P("seq", "head"),
            P("seq", "head"),
            P("seq", "head"),
            P(),
            P(None, "head"),
            P("head"),
            P("seq", "head"),
            P(),
            P("head", "seq"),
            P(),
            P("seq", "head"),
            P("seq", "head"),
            P("head", "seq"),
        ),
        check_vma=False,
    )
```

```python
import functools

import jax
import jax.numpy as jnp
from jax import lax
from jax.experimental import pallas as pl
from jax.experimental.layout import Layout, with_layout_constraint
from jax.experimental.pallas import tpu as pltpu
from jax.sharding import PartitionSpec as P

DK = 256
DV = 512
BLOCK = 128
HALF = BLOCK // 2
EPSILON = 1e-06
LOW = jnp.bfloat16
FULL = jnp.float32
LANES = 128

NN = ((1,), (0,))
TN = ((0,), (0,))
NT = ((1,), (1,))


def dot(left, right, dims=NN):
    return lax.dot_general(left, right, (dims, ((), ())), preferred_element_type=FULL)


def halves(x):
    high = x.astype(LOW)
    return high, (x - high.astype(FULL)).astype(LOW)


def thirds(x):
    high, rest = x.astype(LOW), None
    rest = x - high.astype(FULL)
    middle = rest.astype(LOW)
    return high, middle, (rest - middle.astype(FULL)).astype(LOW)


def fine(left, right, dims=NN):
    (lh, ll), (rh, rl) = left, right
    return dot(lh, rh, dims) + (dot(lh, rl, dims) + dot(ll, rh, dims))


def triangle(lower):
    row = lax.broadcasted_iota(jnp.int32, (BLOCK, BLOCK), 0)
    col = lax.broadcasted_iota(jnp.int32, (BLOCK, BLOCK), 1)
    return row >= col if lower else row <= col


def running_sum(x, lower=True):
    ones = triangle(lower).astype(FULL).astype(LOW)
    high, middle, low = thirds(x)
    return dot(ones, high) + (dot(ones, middle) + dot(ones, low))


def column_sum(x):
    ones = jnp.ones((x.shape[0], LANES), LOW)
    high, middle, low = thirds(x)
    return dot(high, ones, TN) + (dot(middle, ones, TN) + dot(low, ones, TN))


def widen(column, width):
    return jnp.concatenate([column] * (width // LANES), axis=1)


def summary_kernel(info, k_ref, v_ref, decay_ref, out_ref, state, passed, total):
    step, count = pl.program_id(0), pl.num_programs(0)
    at = count - 1 - step

    @pl.when(step == 0)
    def _():
        state[...] = jnp.zeros_like(state)
        passed[...] = jnp.zeros_like(passed)
        total[...] = jnp.zeros_like(total)

    decay = decay_ref[...]
    run = running_sum(decay)
    closing = run[BLOCK - 1 :, :]
    alive = info[1 + count + at].astype(FULL)
    tail = jnp.exp(passed[0:1, :] + closing - run) * (k_ref[...] * alive)
    state[...] += fine(halves(tail), halves(v_ref[...]), TN)
    passed[0:1, :] += closing
    total[...] += column_sum(decay)

    @pl.when(step == count - 1)
    def _():
        out_ref[:, :DV] = state[...].astype(LOW)
        lane = lax.broadcasted_iota(jnp.int32, (DK, LANES), 1)
        high, middle, low = thirds(jnp.exp(total[...]) * info[1 + 3 * count].astype(FULL))
        high, middle, low = high.astype(FULL), middle.astype(FULL), low.astype(FULL)
        out_ref[:, DV:] = jnp.where(lane == 0, high, jnp.where(lane == 1, middle, low)).astype(LOW)


def chain_kernel(backwards, pieces_ref, local_ref, out_ref):
    groups, slab = local_ref.shape[0], local_ref.shape[1]
    current = jnp.zeros((slab, DV), FULL)
    for j in reversed(range(groups)) if backwards else range(groups):
        out_ref[j] = current.astype(LOW)
        through = pieces_ref[j][:, DV:].astype(FULL)
        through = through[:, 0:1] + through[:, 1:2] + through[:, 2:3]
        current = through * current + local_ref[j][:, :DV].astype(FULL)


def chain_call(pieces, local, backwards):
    groups, slab, _ = pieces.shape
    return pl.pallas_call(
        functools.partial(chain_kernel, backwards),
        out_shape=shape_of(groups, slab, DV, dtype=LOW),
        compiler_params=pltpu.CompilerParams(vmem_limit_bytes=40 * 1024 * 1024),
    )(pieces, local)


def mix_kernel(
    info, q_ref, k_ref, v_ref, g_ref, decay_ref, enter_ref, gain_ref, mixed_ref, gated_ref, states_ref, state
):
    step = pl.program_id(0)

    @pl.when(step == 0)
    def _():
        state[...] = enter_ref[...].astype(FULL)

    begin = jnp.where(info[1 + step] > 0, jnp.zeros_like(state), state[...])
    states_ref[0] = begin
    decay = decay_ref[...]
    run = running_sum(decay)
    middle, closing = run[HALF - 1 : HALF, :], run[BLOCK - 1 :, :]
    q = q_ref[...] * DK ** (-0.5)
    k = k_ref[...]
    v = halves(v_ref[...])
    near_q, near_k = halves(q * jnp.exp(run - middle)), halves(k * jnp.exp(middle - run))
    scores = jnp.where(triangle(True), fine(near_q, near_k, NT), 0.0)
    out = fine(halves(q * jnp.exp(run)), halves(begin)) + fine(halves(scores), v)
    tail = halves(k * jnp.exp(closing - run))
    state[...] = widen(jnp.exp(column_sum(decay)), DV) * begin + fine(tail, v, TN)
    mixed_ref[...] = out
    normed = out * lax.rsqrt(jnp.mean(out * out, axis=1, keepdims=True) + EPSILON) * gain_ref[...]
    gate = g_ref[...]
    gated_ref[...] = (normed * (gate * jax.nn.sigmoid(gate))).astype(LOW)


def gate_back_kernel(
    info, q_ref, g_ref, decay_ref, mixed_ref, grad_ref, gain_ref, back_ref, dmixed_ref, out_ref, dgain_ref, state, passed
):
    step, count = pl.program_id(0), pl.num_programs(0)

    @pl.when(step == 0)
    def _():
        state[...] = jnp.zeros_like(state)
        passed[...] = jnp.zeros_like(passed)
        dgain_ref[...] = jnp.zeros_like(dgain_ref)

    mixed, gate, grad, gain = mixed_ref[...], g_ref[...], grad_ref[...], gain_ref[...]
    scale = lax.rsqrt(jnp.mean(mixed * mixed, axis=1, keepdims=True) + EPSILON)
    normed = mixed * scale
    soft = jax.nn.sigmoid(gate)
    back_ref[...] = (grad * (normed * gain) * (soft * (1.0 + gate * (1.0 - soft)))).astype(LOW)
    error = grad * (gate * soft)
    dgain_ref[...] += jnp.sum(error * normed, axis=0, keepdims=True)
    scaled = error * gain
    dmixed = scale * (scaled - normed * jnp.mean(scaled * normed, axis=1, keepdims=True))
    dmixed_ref[...] = dmixed
    run = running_sum(decay_ref[...])
    alive = info[1 + 2 * count + step].astype(FULL)
    reach = jnp.exp(passed[0:1, :] + run) * (q_ref[...] * (DK ** (-0.5) * alive))
    state[...] += fine(halves(reach), halves(dmixed), TN)
    passed[0:1, :] += run[BLOCK - 1 :, :]

    @pl.when(step == count - 1)
    def _():
        out_ref[...] = state[...].astype(LOW)


def mix_back_kernel(
    info,
    q_ref,
    k_ref,
    v_ref,
    decay_ref,
    logits_ref,
    states_ref,
    dmixed_ref,
    leave_ref,
    back_ref,
    dlogits_ref,
    dbias_ref,
    state,
):
    step, count = pl.program_id(0), pl.num_programs(0)
    at = count - 1 - step

    @pl.when(step == 0)
    def _():
        state[...] = leave_ref[...].astype(FULL)
        dbias_ref[...] = jnp.zeros_like(dbias_ref)

    after, begin = state[...], states_ref[0]
    decay = decay_ref[...]
    run = running_sum(decay)
    middle, closing = run[HALF - 1 : HALF, :], run[BLOCK - 1 :, :]
    q, k = q_ref[...] * DK ** (-0.5), k_ref[...]
    grow, shrink = jnp.exp(run - middle), jnp.exp(middle - run)
    from_start, to_end = jnp.exp(run), jnp.exp(closing - run)
    near_q, near_k = halves(q * grow), halves(k * shrink)
    v, dout = halves(v_ref[...]), halves(dmixed_ref[...])
    after_parts = halves(after)
    keep = triangle(True)
    scores = halves(jnp.where(keep, fine(near_q, near_k, NT), 0.0))
    dscores = halves(jnp.where(keep, fine(dout, v, NT), 0.0))
    tail = k * to_end
    dtail = fine(v, after_parts, NT)
    dq = fine(dscores, near_k) * grow + fine(dout, halves(begin), NT) * from_start
    dk = fine(dscores, near_q, TN) * shrink + dtail * to_end
    dv = fine(scores, dout, TN) + fine(halves(tail), after_parts)
    ones = jnp.ones((16, DV), LOW)
    high, low = halves(begin * after)
    across = (dot(ones, high, NT) + dot(ones, low, NT))[0:1, :]
    dclosing = jnp.sum(dtail * tail, axis=0, keepdims=True) + jnp.exp(closing) * across
    ddecay = running_sum(dq * q - dk * k, lower=False) + dclosing
    dlogits = ddecay * jax.nn.sigmoid(-logits_ref[...]) * (1.0 / 16.0)
    dlogits_ref[...] = dlogits
    dbias_ref[...] += jnp.sum(dlogits, axis=0, keepdims=True)
    back_ref[:, :DV] = dv.astype(LOW)
    back_ref[:, DV : DV + DK] = dk.astype(LOW)
    back_ref[:, DV + DK :] = (dq * DK ** (-0.5)).astype(LOW)
    before = widen(jnp.exp(column_sum(decay)), DV) * after + fine(halves(q * from_start), dout, TN)
    state[...] = jnp.where(info[1 + at] > 0, jnp.zeros_like(before), before)


PARAMS = pltpu.CompilerParams(
    dimension_semantics=("arbitrary",), vmem_limit_bytes=40 * 1024 * 1024
)
QUICK = pl.CostEstimate(flops=1, bytes_accessed=1, transcendentals=0)


def token_call(kernel, info, count, quarter, reverse, inputs, outputs, scratch):
    per = quarter // BLOCK

    def place(i):
        return count - 1 - i if reverse else i

    def spec(shape, column):
        if column is None:
            return pl.BlockSpec(shape, lambda i, info: (0, 0))
        if column == "state":
            return pl.BlockSpec(shape, lambda i, info: (place(i), 0, 0))

        def index(i, info):
            j = place(i)
            return ((j // per) ^ info[0]) * per + j % per, column

        return pl.BlockSpec(shape, index)

    return pl.pallas_call(
        kernel,
        grid_spec=pltpu.PrefetchScalarGridSpec(
            num_scalar_prefetch=1,
            grid=(count,),
            in_specs=[spec(shape, column) for _, shape, column in inputs],
            out_specs=[spec(shape, column) for _, shape, column in outputs],
            scratch_shapes=scratch,
        ),
        out_shape=[out for out, _, _ in outputs],
        compiler_params=PARAMS,
        cost_estimate=QUICK,
    )(info, *[array for array, _, _ in inputs])


def shape_of(*extent, dtype=FULL):
    return jax.ShapeDtypeStruct(extent, dtype)


def fill(piece_refs, places, weight_refs, spans):
    for (piece, source, target, size), (start, stop), weight in (
        (place, span, weight) for place in places for span, weight in zip(spans, weight_refs)
    ):
        weight[target : target + size, :] = piece_refs[piece][source : source + size, start:stop]


def assemble_kernel(places, spans, dotted, x_ref, *refs):
    number = 1 + max(p[0] for p in places)
    pieces, y_ref, weights = refs[:number], refs[number], refs[number + 1 :]

    @pl.when(pl.program_id(0) == 0)
    def _():
        fill(pieces, places, weights, spans)

    for i in range(dotted):
        start, stop = spans[i]
        y_ref[:, start:stop] = dot(x_ref[...], weights[i][...])


def assemble_back_kernel(places, x_ref, pre_ref, *refs):
    number = 1 + max(p[0] for p in places)
    pieces, back_ref, weight = refs[:number], refs[number], refs[number + 1]
    ff = weight.shape[1]

    @pl.when(pl.program_id(0) == 0)
    def _():
        fill(pieces, places, [weight], [(0, ff)])

    grad = dot(x_ref[...], weight[...])
    pre, up = pre_ref[:, :ff], pre_ref[:, ff:]
    soft = jax.nn.sigmoid(pre)
    back_ref[:, :ff] = (grad * up * (soft * (1.0 + pre * (1.0 - soft)))).astype(LOW)
    back_ref[:, ff:] = (grad * (pre * soft)).astype(LOW)


def assemble_gate_kernel(places, x_ref, *refs):
    number = 1 + max(p[0] for p in places)
    pieces, pre_ref, weight, inner_ref = refs[:number], *refs[number:]
    ff = weight.shape[1] // 2

    @pl.when(pl.program_id(0) == 0)
    def _():
        fill(pieces, places, [weight], [(0, 2 * ff)])

    pre_ref[...] = dot(x_ref[...], weight[...])
    gate = pre_ref[:, :ff]
    inner_ref[...] = (gate * jax.nn.sigmoid(gate) * pre_ref[:, ff:]).astype(LOW)


def product_kernel(number, *refs):
    kept_ref, sent_ref = refs[2 * number :]
    total = 0.0
    for x_ref, w_ref in zip(refs[:number], refs[number : 2 * number]):
        total = total + dot(x_ref[...], w_ref[...], NT)
    half = kept_ref.shape[0]
    kept_ref[...] = total[:half]
    sent_ref[...] = total[half:].astype(LOW)


def product_call(pairs, block, half):
    tile = 512
    width = pairs[0][1].shape[0]
    out = pl.BlockSpec((half, tile), lambda i: (0, i))
    return pl.pallas_call(
        functools.partial(product_kernel, len(pairs)),
        grid=(width // tile,),
        in_specs=[
            pl.BlockSpec((2 * half, x.shape[1]), lambda i: (block, 0), pipeline_mode=pl.Buffered(1))
            for x, _ in pairs
        ]
        + [pl.BlockSpec((tile, w.shape[1]), lambda i: (i, 0)) for _, w in pairs],
        out_specs=[out, out],
        out_shape=[shape_of(half, width), shape_of(half, width, dtype=LOW)],
        compiler_params=PARAMS,
        cost_estimate=QUICK,
    )(*[x for x, _ in pairs], *[w for _, w in pairs])


def parts_kernel(number, targets, wide, table, *refs):
    outs = refs[2 * number :]
    values = [dot(l[...], r[...], TN) for l, r in zip(refs[:number], refs[number : 2 * number])]
    for step, (target, row) in enumerate(targets):

        @pl.when(pl.program_id(0) == step)
        def _():
            start = 0
            for value in values:
                stop = start + value.shape[1]
                outs[target][row * wide : (row + 1) * wide, start:stop] = value.astype(outs[target].dtype)
                start = stop


def parts_call(pairs, groups, wide, dtype):
    columns = sum(r.shape[1] for _, r in pairs)
    if wide % LANES:
        def part(k):
            cut = slice(k * wide, (k + 1) * wide)
            return jnp.concatenate([dot(l[:, cut], r, TN) for l, r in pairs], axis=1)

        return [jnp.concatenate([part(k) for k in group], axis=0).astype(dtype) for group in groups]
    flat = [(j, i, k) for j, group in enumerate(groups) for i, k in enumerate(group)]

    def fixed(shape):
        return pl.BlockSpec(shape, lambda i, table: (0, 0), pipeline_mode=pl.Buffered(1))

    return pl.pallas_call(
        functools.partial(parts_kernel, len(pairs), [(j, i) for j, i, _ in flat], wide),
        grid_spec=pltpu.PrefetchScalarGridSpec(
            num_scalar_prefetch=1,
            grid=(len(flat),),
            in_specs=[pl.BlockSpec((l.shape[0], wide), lambda i, table: (0, table[i])) for l, _ in pairs]
            + [fixed(r.shape) for _, r in pairs],
            out_specs=[fixed((len(g) * wide, columns)) for g in groups],
        ),
        out_shape=[shape_of(len(g) * wide, columns, dtype=dtype) for g in groups],
        compiler_params=PARAMS,
        cost_estimate=QUICK,
    )(jnp.asarray([k for _, _, k in flat], jnp.int32), *[l for l, _ in pairs], *[r for _, r in pairs])


def once(shape):
    return pl.BlockSpec(shape, lambda i: (0, 0), pipeline_mode=pl.Buffered(1))


def assemble_call(kernel, x, extra, pieces, out_width, out_dtype, spans, depth, also=None):
    tile = 256
    rows = lambda width: pl.BlockSpec((tile, width), lambda i: (i, 0))
    return pl.pallas_call(
        kernel,
        grid=(x.shape[0] // tile,),
        in_specs=[rows(x.shape[1])]
        + [rows(e.shape[1]) for e in extra]
        + [once(p.shape) for p in pieces],
        out_specs=[rows(out_width)]
        + [once((depth, stop - start)) for start, stop in spans]
        + ([rows(also)] if also else []),
        out_shape=[shape_of(x.shape[0], out_width, dtype=out_dtype)]
        + [shape_of(depth, stop - start, dtype=LOW) for start, stop in spans]
        + ([shape_of(x.shape[0], also, dtype=LOW)] if also else []),
        compiler_params=pltpu.CompilerParams(
            dimension_semantics=("arbitrary",), vmem_limit_bytes=52 * 1024 * 1024
        ),
        cost_estimate=QUICK,
    )(x, *extra, *pieces)


def columns_in_kernel(order, core, a, b, c, d, oa, ob, oc, od):
    oa[...] = a[...]
    ob[...] = b[...]
    oc[...] = c[...]
    od[...] = d[...]


def columns_in(hidden, cotangent, gain_a, gain_b, order, core, quarter, wide):
    count = order.shape[0]
    if wide % LANES:
        def pick(x):
            return jnp.concatenate(
                [lax.dynamic_slice_in_dim(x, order[i] * wide, wide, 1) for i in range(count)], axis=1
            )

        def rows(x):
            return lax.dynamic_slice_in_dim(x, core * quarter, quarter, 0)

        return pick(rows(hidden)), pick(rows(cotangent)), pick(gain_a), pick(gain_b)
    big = pl.BlockSpec((quarter, wide), lambda i, order, core: (core[0], order[i]))
    small = pl.BlockSpec((1, wide), lambda i, order, core: (0, order[i]))
    big_out = pl.BlockSpec((quarter, wide), lambda i, order, core: (0, i))
    small_out = pl.BlockSpec((1, wide), lambda i, order, core: (0, i))
    total = count * wide
    return pl.pallas_call(
        columns_in_kernel,
        grid_spec=pltpu.PrefetchScalarGridSpec(
            num_scalar_prefetch=2,
            grid=(count,),
            in_specs=[big, big, small, small],
            out_specs=[big_out, big_out, small_out, small_out],
        ),
        out_shape=[
            shape_of(quarter, total, dtype=LOW),
            shape_of(quarter, total, dtype=LOW),
            shape_of(1, total),
            shape_of(1, total),
        ],
        compiler_params=PARAMS,
    )(order, core.reshape(1), hidden, cotangent, gain_a, gain_b)


def columns_out_kernel(order, core, mine, near, out):
    quarter = mine.shape[0]
    first = core[0] == 0
    out[:quarter, :] = jnp.where(first, mine[...], near[...])
    out[quarter:, :] = jnp.where(first, near[...], mine[...])


def columns_out(mine, near, order, inverse, core, wide):
    quarter, total = mine.shape
    count = order.shape[0]
    if wide % LANES:
        first = core == 0
        both = jnp.concatenate([jnp.where(first, mine, near), jnp.where(first, near, mine)], axis=0)
        return jnp.concatenate(
            [lax.dynamic_slice_in_dim(both, inverse[i] * wide, wide, 1) for i in range(count)], axis=1
        )
    spec = pl.BlockSpec((quarter, wide), lambda i, order, core: (0, i))
    return pl.pallas_call(
        columns_out_kernel,
        grid_spec=pltpu.PrefetchScalarGridSpec(
            num_scalar_prefetch=2,
            grid=(count,),
            in_specs=[spec, spec],
            out_specs=pl.BlockSpec((2 * quarter, wide), lambda i, order, core: (0, order[i])),
        ),
        out_shape=shape_of(2 * quarter, total, dtype=mine.dtype),
        compiler_params=PARAMS,
    )(order, core.reshape(1), mine, near)


def block_resets(lengths, dealing, count, start):
    number = lengths.shape[0]
    picks = (dealing[:, None] == jnp.arange(number, dtype=jnp.int32)[None, :]).astype(jnp.int32)
    placed = jnp.sum(picks * lengths[None, :], axis=1, dtype=jnp.int32)
    ends = jnp.cumsum(placed, dtype=jnp.int32)
    starts = ends - placed
    firsts = start + jnp.arange(count, dtype=jnp.int32)
    return jnp.any(firsts[:, None] == starts[None, :], axis=1).astype(jnp.int32)


def tied(*values):
    return lax.optimization_barrier(values)


def silu(x):
    return x * jax.nn.sigmoid(x)


def shards(
    hidden_in,
    cotangent,
    lengths,
    dealing,
    norm_attn,
    w_query,
    w_key,
    w_value,
    w_rank_in,
    w_rank_out,
    decay_bias,
    w_gate_out,
    head_gain,
    w_out,
    norm_mlp,
    w_ff_gate,
    w_ff_up,
    w_ff_down,
):
    peers = lax.axis_size("seq")
    place, core = lax.axis_index("seq"), lax.axis_index("head")
    laps, groups = peers // 4, peers // 2
    group, left = place // 2, place % 2 == 0
    rows, width = hidden_in.shape
    quarter = rows // 2
    tokens = 4 * quarter
    count = tokens // BLOCK
    wide = width // groups
    ff = w_ff_gate.shape[1] // 2

    def pair(x):
        return lax.ppermute(x, "seq", [(i, i ^ 1) for i in range(peers)])

    def side(x):
        return lax.ppermute(x, "seq", [(i, i ^ 2) for i in range(peers)])

    def ring(x):
        return lax.ppermute(x, "seq", [(i, (i + 4) % peers) for i in range(peers)])

    def twin(x):
        return lax.ppermute(x, "head", [(0, 1), (1, 0)])

    lap, flank = group // 2, group % 2
    steps = jnp.arange(groups, dtype=jnp.int32)
    order = ((lap - steps % laps) % laps) * 2 + (flank ^ (steps // laps))
    inverse = (flank ^ (steps % 2)) * laps + (lap - steps // 2) % laps
    resets = block_resets(lengths, dealing, count, group * count)
    ahead = jnp.cumsum(resets)
    info = jnp.concatenate(
        [
            ((place % 2) * 2 + core).astype(jnp.int32).reshape(1),
            resets,
            (ahead == ahead[-1]).astype(jnp.int32),
            (ahead == 0).astype(jnp.int32),
            (ahead[-1:] == 0).astype(jnp.int32),
        ]
    )

    def split(*arrays):
        mid = [a.shape[1] // 2 for a in arrays]
        low = jnp.concatenate([a[:, :m] for a, m in zip(arrays, mid)], axis=1)
        high = jnp.concatenate([a[:, m:] for a, m in zip(arrays, mid)], axis=1)
        return jnp.where(left, low, high), jnp.where(left, high, low)

    def turned_over(x):
        return with_layout_constraint(x.T, Layout((0, 1)))

    def joined(mine, got):
        return jnp.concatenate(
            [jnp.where(left, mine, got), jnp.where(left, got, mine)], axis=0
        )

    class Gather:
        def __init__(self, own):
            self.blocks, self.others = [own], []

        def ring(self):
            if len(self.blocks) < laps:
                self.blocks.append(ring(self.blocks[-1]))

        def side(self, number=1):
            for _ in range(number):
                if len(self.others) < min(laps, len(self.blocks)):
                    self.others.append(side(self.blocks[len(self.others)]))

        def rest(self):
            while len(self.blocks) < laps:
                self.ring()

        def pieces(self):
            arrays = self.blocks + self.others
            return arrays, [(i, 0, i * wide, wide) for i in range(len(arrays))]

    class GatherSide(Gather):
        def begin(self):
            self.got = side(self.blocks[0])

        def join(self):
            self.blocks = [jnp.concatenate([self.blocks[0], self.got], axis=0)]

        def pieces(self):
            places = [(i, 0, i * wide, wide) for i in range(laps)]
            places += [(i, wide, (laps + i) * wide, wide) for i in range(laps)]
            return self.blocks, places

    class Reduce:
        def __init__(self, *pairs):
            self.pairs = pairs
            self.turn = [(p + 1) % laps for p in range(laps)]
            self.parts, self.owns, self.sent, self.flown = [], [], [], None
            self.done = 0

        def make(self):
            self.parts = list(parts_call(self.pairs, [[laps + p] for p in self.turn], wide, LOW))

        def make_own(self):
            self.owns = list(parts_call(self.pairs, [[p] for p in self.turn], wide, FULL))

        def send(self, number=1):
            for _ in range(number):
                if len(self.sent) < laps:
                    self.sent.append(side(self.parts[len(self.sent)]))

        def add(self):
            while len(self.sent) <= self.done:
                self.send()
            value = self.owns[self.done] + self.sent[self.done]
            if self.flown is not None:
                value = value + self.flown
            self.done += 1
            return value

        def ready(self):
            self.value = self.add().astype(LOW)

        def fly(self):
            self.flown = ring(self.value)

        def hop(self):
            if self.done < laps - 1:
                self.ready()
                self.fly()

        def last(self):
            while self.done < laps - 1:
                self.hop()
            self.total = self.add()

        def halve(self):
            total = self.total
            top, low = total[: wide // 2], total[wide // 2 :]
            self.mine = jnp.where(left, top, low)
            self.got = pair(jnp.where(left, low, top).astype(LOW))

        def out(self):
            got = self.got.astype(FULL)
            return jnp.where(left, self.mine, got), jnp.where(left, got, self.mine)

    class ReduceSide(Reduce):
        def make(self):
            p = self.turn[0]
            (self.value,) = parts_call(self.pairs, [[p, laps + p]], wide, LOW)

        def make_own(self):
            self.owns = [None] + list(
                parts_call(self.pairs, [[p, laps + p] for p in self.turn[1:]], wide, FULL)
            )

        def begin(self):
            self.done = 1
            self.fly()

        def add(self):
            value = self.owns[self.done] + self.flown
            self.done += 1
            return value

        def cross(self):
            while self.done < laps - 1:
                self.hop()
            total = self.add()
            self.kept = total[:wide]
            self.come = side(total[wide:].astype(LOW))

        def last(self):
            self.total = self.kept + self.come

    def together(*things):
        def read(holder, key):
            return holder[key] if isinstance(key, int) else getattr(holder, key)

        values = [read(*t) if isinstance(t, tuple) else t for t in things]
        values = lax.optimization_barrier(values)
        back = []
        for thing, value in zip(things, values):
            if not isinstance(thing, tuple):
                back.append(value)
            elif isinstance(thing[1], int):
                thing[0][thing[1]] = value
            else:
                setattr(*thing, value)
        return back[0] if len(back) == 1 else back

    def spread_near(x):
        return pair(x), twin(x)

    def spread_all(x, far, near, other):
        return jnp.concatenate([x, near, far, other], axis=0)

    q2 = 2 * quarter

    def far_part(*pairs):
        return list(product_call(pairs, 1, quarter))

    def near_part(*pairs):
        return list(product_call(pairs, 0, quarter))

    def summed_pair(kept, sent):
        return kept + twin(sent)

    mine, other = split(w_value, w_key)
    got = pair(other)
    hidden_low, cot_own, gain_attn, gain_mlp = columns_in(
        hidden_in, cotangent, norm_attn[None], norm_mlp[None], order, core, quarter, wide
    )
    hidden = hidden_low.astype(FULL)
    scale_attn = lax.rsqrt(jnp.mean(hidden * hidden, axis=1, keepdims=True) + EPSILON)
    first_own = (hidden * scale_attn * gain_attn).astype(LOW)
    got, first_own, cot_own, w_rank_in, w_gate_out, w_query, w_out = together(
        got, first_own, cot_own, w_rank_in, w_gate_out, w_query, w_out
    )
    keys = Gather(joined(mine, got))
    keys.ring()
    keys.side()
    far, near = spread_near(first_own)
    mine, other = split(w_gate_out, w_query, turned_over(w_out))
    mine, other, w_ff_gate, w_ff_up, w_ff_down, w_rank_in = together(
        mine, other, (keys.blocks, 1), w_ff_gate, w_ff_up, w_ff_down, w_rank_in
    )
    keys.ring()
    keys.side()
    got = pair(other)
    mine_b, other_b = split(w_ff_gate, w_ff_up)
    mine_d, other_d = split(turned_over(w_ff_down))
    rank_weight = jnp.concatenate(
        [lax.dynamic_slice_in_dim(w_rank_in, order[i] * wide, wide, 0) for i in range(groups)], axis=0
    )
    far, near, mine_b, other_b, mine_d, other_d, rank_weight = together(
        (keys.blocks, 2), (keys.others, 0), far, near, mine_b, other_b, mine_d, other_d, rank_weight
    )
    keys.rest()
    keys.side()
    other = twin(far)
    first = spread_all(first_own, far, near, other)
    first, got, other_b, other_d = together(
        (keys.blocks, laps - 1), (keys.others, 1), first, got, other_b, other_d
    )
    keys.side(laps)
    got_d = pair(other_d)
    gates = Gather(joined(mine, got))
    gates.ring()
    rank_in = dot(first, rank_weight).astype(LOW)
    rank_out = jnp.where(left, w_rank_out[:, :DK], w_rank_out[:, DK:])
    bias = jnp.where(left, decay_bias[:DK], decay_bias[DK:])
    logits = dot(rank_in, rank_out) + bias
    decay = jax.nn.log_sigmoid(logits) / 16.0
    first, rank_in, decay, logits, got_d = together(
        *[(keys.others, i) for i in range(2, laps)],
        (gates.blocks, 0),
        (gates.blocks, 1),
        first,
        rank_in,
        decay,
        logits,
        got_d,

    )
    got_b = pair(other_b)
    gates.ring()
    gates.side()
    downs = GatherSide(joined(mine_d, got_d))
    downs.begin()
    arrays, places = keys.pieces()
    span = [(0, DV + DK)]
    keyed, full_k = assemble_call(
        functools.partial(assemble_kernel, places, span, 1), first, [], arrays, DV + DK, FULL, span, width
    )
    gain = head_gain[None]
    state_scratch = pltpu.VMEM((DK, DV), FULL)
    row_scratch = pltpu.VMEM((8, DK), FULL)
    key_block, val_block = (BLOCK, DK), (BLOCK, DV)
    state_shape = (DK, DV)
    call = functools.partial(token_call, info=info, count=count, quarter=quarter)
    (summary,) = call(
        summary_kernel,
        reverse=True,
        inputs=[(keyed, key_block, 2), (keyed, val_block, 0), (decay, key_block, 0)],
        outputs=[(shape_of(DK, DV + LANES, dtype=LOW), (DK, DV + LANES), None)],
        scratch=[state_scratch, row_scratch, pltpu.VMEM((DK, LANES), FULL)],
    )
    summary, got_b, downs.blocks[0] = together(
        (gates.blocks, 2), (gates.others, 0), (downs, "got"), summary, got_b, downs.blocks[0]
    )
    gates.rest()
    gates.side()
    halves_of_seq = [[i for i in range(peers) if i % 2 == k] for k in range(2)]
    slab = DK // groups

    def turned(x):
        return lax.all_to_all(x, "seq", 0, 0, axis_index_groups=halves_of_seq, tiled=True)

    pieces = turned(summary).reshape(groups, slab, DV + LANES)
    ffs = Gather(joined(mine_b, got_b))
    downs.join()
    cot_far, cot_near = spread_near(cot_own)
    pieces, ffs.blocks[0], cot_far, cot_near = together(
        (gates.blocks, laps - 1),
        (gates.others, 1),
        (downs.blocks, 0),
        pieces,
        ffs.blocks[0],
        cot_far,
        cot_near,
    )
    gates.side(laps)
    ffs.ring()
    cot_other = twin(cot_far)
    entering = turned(chain_call(pieces, pieces, False).reshape(DK, DV))
    entering, keyed, first, cot_other, downs.blocks[0] = together(
        *[(gates.others, i) for i in range(2, laps)],
        (ffs.blocks, 1),
        entering,
        keyed,
        first,
        cot_other,
        downs.blocks[0],
    )
    ffs.ring()
    ffs.side()
    cot = spread_all(cot_own, cot_far, cot_near, cot_other)
    arrays, places = gates.pieces()
    span = [(0, DV), (DV, DV + DK), (DV + DK, 2 * DV + DK)]
    gated_in, full_g, full_q, full_o = assemble_call(
        functools.partial(assemble_kernel, places, span, 2), first, [], arrays, DV + DK, FULL, span, width
    )
    mixed, gated, states = call(
        mix_kernel,
        reverse=False,
        inputs=[
            (gated_in, key_block, 2),
            (keyed, key_block, 2),
            (keyed, val_block, 0),
            (gated_in, val_block, 0),
            (decay, key_block, 0),
            (entering, state_shape, None),
            (gain, (1, DV), None),
        ],
        outputs=[
            (shape_of(tokens, DV), val_block, 0),
            (shape_of(tokens, DV, dtype=LOW), val_block, 0),
            (shape_of(count, DK, DV), (1, DK, DV), "state"),
        ],
        scratch=[state_scratch],
    )

    gated, cot = together((ffs.blocks, 2), (ffs.others, 0), gated, cot)
    far, gated = together(summed_pair(*far_part((gated, full_o))).astype(LOW), gated)
    ffs.rest()
    ffs.side()
    got = pair(far)
    near = near_part((gated, full_o))
    got, near = together((ffs.blocks, laps - 1), (ffs.others, 1), got, near)
    resid = hidden + (summed_pair(*near) + got)
    scale_mlp = lax.rsqrt(jnp.mean(resid * resid, axis=1, keepdims=True) + EPSILON)
    second_own = together((resid * scale_mlp * gain_mlp).astype(LOW))
    ffs.side()
    downs.ring()
    far, near = spread_near(second_own)
    far, near, second_own = together(
        (ffs.others, 2), (downs.blocks, 1), far, near, second_own
    )
    ffs.side(laps)
    downs.ring()
    other = twin(far)
    second = spread_all(second_own, far, near, other)
    second, cot = together(*[(ffs.others, i) for i in range(3, laps)], (downs.blocks, 2), second, cot)
    downs.rest()
    arrays, places = ffs.pieces()
    span = [(0, 2 * ff)]
    ff_both, full_f, inner = assemble_call(
        functools.partial(assemble_gate_kernel, places), second, [], arrays, 2 * ff, FULL, span, width, ff
    )
    down_grad = ReduceSide((cot, inner))
    down_grad.make()
    down_grad.make_own()
    inner, ff_both, cot, second = together(
        (downs.blocks, laps - 1), (down_grad, "value"), (down_grad, "owns"), inner, ff_both, cot, second
    )
    down_grad.begin()
    down_grad.pairs = ((cot, inner),)
    arrays, places = downs.pieces()
    both_back, full_d = assemble_call(
        functools.partial(assemble_back_kernel, places), cot, [ff_both], arrays, 2 * ff, LOW, [(0, ff)], width
    )

    gate_grad = Reduce((second, both_back[:, :ff]))
    gate_grad.make()
    far = far_part((both_back, full_f))
    far, both_back, second, full_d, full_f, inner, cot = together(
        (down_grad, "flown"), (gate_grad, "parts"), far, both_back, second, full_d, full_f, inner, cot
    )
    far, both_back, second, full_f, inner, cot, down_grad.flown = together(
        summed_pair(*far).astype(LOW), both_back, second, full_f, inner, cot, down_grad.flown
    )
    down_grad.pairs = ((cot, inner),)
    gate_grad.pairs = ((second, both_back[:, :ff]),)
    got = pair(far)
    gate_grad.send(2)
    down_grad.hop()
    near = near_part((both_back, full_f))
    up_grad = Reduce((second, both_back[:, ff:]))
    up_grad.make()
    got, near, both_back, second = together(
        (down_grad, "flown"),
        (up_grad, "parts"),
        (gate_grad.sent, 0),
        (gate_grad.sent, 1),
        got,
        near,
        both_back,
        second,
    )
    gate_grad.pairs = ((second, both_back[:, :ff]),)
    up_grad.pairs = ((second, both_back[:, ff:]),)

    def norm_back(grad, value, scale, gains):
        normed = value * scale
        scaled = grad * gains
        gain_grad = jnp.sum(grad * normed, axis=0, keepdims=True)
        return scale * (scaled - normed * jnp.mean(scaled * normed, axis=1, keepdims=True)), gain_grad

    resid_norm, grad_gain_mlp = norm_back(summed_pair(*near) + got, resid, scale_mlp, gain_mlp)
    grad_resid = cot_own.astype(FULL) + resid_norm
    back_own, both_back, second, down_grad.owns, down_grad.flown = together(
        grad_resid.astype(LOW), both_back, second, down_grad.owns, down_grad.flown
    )
    gate_grad.pairs = ((second, both_back[:, :ff]),)
    up_grad.pairs = ((second, both_back[:, ff:]),)
    far, near = spread_near(back_own)
    gate_grad.send(laps)
    down_grad.hop()
    gate_grad.make_own()
    up_grad.make_own()
    far, near, back_own = together(
        (gate_grad, "owns"),
        (up_grad, "owns"),
        (down_grad, "flown"),
        *[(gate_grad.sent, i) for i in range(2, laps)],
        far,
        near,
        back_own,
    )
    other = twin(far)
    resid_back, full_d, inner, full_o, gate_grad.sent[0] = together(
        spread_all(back_own, far, near, other), full_d, inner, full_o, gate_grad.sent[0]
    )
    up_grad.send()
    gate_grad.hop()
    grad_gated = dot(resid_back, full_o)
    gate_back, dmixed, summary_back, grad_gain_head = call(
        gate_back_kernel,
        reverse=False,
        inputs=[
            (gated_in, key_block, 2),
            (gated_in, val_block, 0),
            (decay, key_block, 0),
            (mixed, val_block, 0),
            (grad_gated, val_block, 0),
            (gain, (1, DV), None),
        ],
        outputs=[
            (shape_of(tokens, DV, dtype=LOW), val_block, 0),
            (shape_of(tokens, DV), val_block, 0),
            (shape_of(DK, DV, dtype=LOW), state_shape, None),
            (shape_of(1, DV), (1, DV), None),
        ],
        scratch=[state_scratch, row_scratch],
    )
    summary_back, resid_back, gate_back, first, gated = together(
        (up_grad.sent, 0),
        (up_grad, "parts"),
        (down_grad, "flown"),
        (gate_grad, "flown"),
        summary_back,
        resid_back,
        gate_back,
        first,
        gated,
    )
    up_grad.send()
    gate_grad.hop()
    pieces_back = turned(summary_back).reshape(groups, slab, DV)
    out_grad = Reduce((resid_back, gated), (first, gate_back))
    out_grad.make()
    up_grad.ready()
    pieces_back, full_d, inner, resid_back, gate_back, first, gated = together(
        (up_grad.sent, 1),
        (up_grad, "parts"),
        (down_grad, "flown"),
        (gate_grad, "flown"),
        (out_grad, "parts"),
        (up_grad, "value"),
        pieces_back,
        full_d,
        inner,
        resid_back,
        gate_back,
        first,
        gated,
    )
    leaving, gate_grad.flown, up_grad.sent[0] = together(
        chain_call(pieces, pieces_back, True), gate_grad.flown, up_grad.sent[0]
    )
    out_grad.pairs = ((resid_back, gated), (first, gate_back))
    up_grad.send()
    up_grad.fly()
    out_grad.make_own()
    leaving = turned(leaving.reshape(DK, DV))
    out_far, out_near = far_part((inner, full_d)), near_part((inner, full_d))
    leaving, keyed, out_far, out_near = together(
        (up_grad, "flown"),
        (out_grad, "owns"),
        (out_grad, "parts"),
        (up_grad.sent, 2),
        (up_grad, "parts"),
        (down_grad, "flown"),
        leaving,
        keyed,
        out_far,
        out_near,
    )
    out_grad.send(2)
    gate_grad.hop()
    mixes_back, grad_logits, grad_bias = call(
        mix_back_kernel,
        reverse=True,
        inputs=[
            (gated_in, key_block, 2),
            (keyed, key_block, 2),
            (keyed, val_block, 0),
            (decay, key_block, 0),
            (logits, key_block, 0),
            (states, (1, DK, DV), "state"),
            (dmixed, val_block, 0),
            (leaving, state_shape, None),
        ],
        outputs=[
            (shape_of(tokens, DV + 2 * DK, dtype=LOW), (BLOCK, DV + 2 * DK), 0),
            (shape_of(tokens, DK), key_block, 0),
            (shape_of(1, DK), (1, DK), None),
        ],
        scratch=[state_scratch],
    )
    mixes_back, grad_logits, first, resid_back, gate_back, full_k, full_q, full_g = together(
        (gate_grad, "flown"),
        (out_grad.sent, 0),
        (up_grad, "parts"),
        (down_grad, "flown"),
        mixes_back,
        grad_logits,
        first,
        resid_back,
        gate_back,
        full_k,
        full_q,
        full_g,
    )
    out_grad.pairs = ((resid_back, gated), (first, gate_back))
    up_grad.send(laps)
    up_grad.hop()
    down_grad.cross()
    mix_grad = Reduce((first, mixes_back))
    mix_grad.make()
    full_vkq = jnp.concatenate([full_k, full_q], axis=1)
    precise = lax.Precision.HIGHEST
    grad_rank = lax.dot_general(
        grad_logits, rank_out.astype(FULL), (NT, ((), ())), precision=precise
    )
    rank_high = grad_rank.astype(LOW)
    rank_low = (grad_rank - rank_high.astype(FULL)).astype(LOW)

    back_pairs = (
        (mixes_back, full_vkq),
        (gate_back, full_g),
        (rank_high, rank_weight),
        (rank_low, rank_weight),
    )
    far = far_part(*back_pairs)
    far, first, back_pairs, resid_back, gate_back, gated = together(
        (out_grad.sent, 1),
        (up_grad, "flown"),
        (mix_grad, "parts"),
        far,
        first,
        list(back_pairs),
        resid_back,
        gate_back,
        gated,
    )
    up_grad.ready()
    out_grad.ready()
    far, first, back_pairs, grad_logits, out_far, out_near = together(
        (up_grad, "value"),
        (out_grad, "value"),
        summed_pair(*far).astype(LOW),
        first,
        back_pairs,
        grad_logits,
        out_far,
        out_near,
    )
    mixes_back, rank_high, rank_low = back_pairs[0][0], back_pairs[2][0], back_pairs[3][0]
    mix_grad.pairs = ((first, mixes_back),)
    got = pair(far)
    out_grad.send()
    mix_grad.send()
    out_grad.fly()
    up_grad.fly()
    near = near_part(*back_pairs)
    mix_grad.make_own()
    got, near, rank_high, rank_low, first, rank_in, grad_logits, out_far, out_near = together(
        *[(up_grad.sent, i) for i in range(3, laps)],
        (down_grad, "come"),
        (out_grad.sent, 2),
        (mix_grad.sent, 0),
        (mix_grad, "owns"),
        (out_grad, "flown"),
        (up_grad, "flown"),
        got,
        near,
        rank_high,
        rank_low,
        first,
        rank_in,
        grad_logits,
        out_far,
        out_near,
    )
    out_far, out_near = summed_pair(*out_far).astype(LOW), summed_pair(*out_near)
    mix_grad.send()
    mix_grad.hop()
    out_grad.send(laps)
    out_grad.hop()
    grad_rank_in = dot(rank_high, first, TN) + dot(rank_low, first, TN)
    grad_rank_out = lax.dot_general(
        rank_in.astype(FULL), grad_logits, (TN, ((), ())), precision=precise
    )
    hidden_norm, grad_gain_attn = norm_back(summed_pair(*near) + got, hidden, scale_attn, gain_attn)
    input_own = grad_resid + hidden_norm
    input_own, grad_gain_attn = together(
        (mix_grad.sent, 1), (mix_grad, "flown"), (out_grad, "flown"), input_own, grad_gain_attn
    )
    out_got = pair(out_far)
    mix_grad.send(laps)
    mix_grad.hop()
    down_grad.last()
    down_grad.halve()
    input_near = twin(input_own)

    def unordered(x):
        return jnp.concatenate(
            [lax.dynamic_slice_in_dim(x, inverse[i] * wide, wide, 1) for i in range(groups)], axis=1
        )

    wide_part = jnp.concatenate(
        [grad_rank_in, grad_gain_attn, grad_gain_mlp, jnp.zeros((6, width), FULL)], axis=0
    )
    wide_part = unordered(wide_part + twin(wide_part))
    empty = jnp.zeros_like(grad_rank_out)
    rank_part = jnp.concatenate(
        [jnp.where(left, grad_rank_out, empty), jnp.where(left, empty, grad_rank_out)], axis=1
    )
    bias_part = jnp.concatenate(
        [jnp.where(left, grad_bias, 0.0), jnp.where(left, 0.0, grad_bias)], axis=1
    )
    head_part = grad_gain_head + twin(grad_gain_head)
    narrow_part = jnp.concatenate(
        [rank_part, bias_part, head_part, jnp.zeros((6, 2 * DK), FULL)], axis=0
    )
    small = jnp.concatenate([wide_part, narrow_part], axis=1)
    input_near, small, out_got = together(
        (mix_grad.sent, 2), (mix_grad, "flown"), (down_grad, "got"), input_near, small, out_got
    )
    hops = [1 << k for k in (0, *range(2, peers.bit_length() - 1), 1)]

    def summed(small):
        hop = hops.pop(0)
        return small + lax.ppermute(small, "seq", [(i, i ^ hop) for i in range(peers)])

    mix_grad.hop()
    out_grad.hop()
    small = summed(small)
    gate_grad.last()
    gate_grad.halve()
    grad_input = columns_out(input_own, input_near, order, inverse, core, wide)
    small, grad_input = together(
        *[(mix_grad.sent, i) for i in range(3, laps)],
        (mix_grad, "flown"),
        (out_grad, "flown"),
        (gate_grad, "got"),
        small,
        grad_input,
    )
    mix_grad.last()
    mix_grad.halve()
    small = summed(small)
    small = together((mix_grad, "got"), small)
    small = summed(small)
    up_grad.last()
    up_grad.halve()
    small = together((up_grad, "got"), small)
    out_grad.last()
    out_grad.halve()
    out_own = (resid + (out_near + out_got)).astype(LOW)
    block_out = columns_out(out_own, twin(out_own), order, inverse, core, wide)
    while hops:
        small = summed(small)
    down_halves, gate_halves, up_halves = down_grad.out(), gate_grad.out(), up_grad.out()
    out_halves, mix_halves = out_grad.out(), mix_grad.out()

    def beside(pieces, start, stop):
        return jnp.concatenate([half[:, start:stop] for half in pieces], axis=1)

    return (
        block_out,
        grad_input,
        small[16, :width],
        beside(mix_halves, DV + DK, DV + 2 * DK),
        beside(mix_halves, DV, DV + DK),
        beside(mix_halves, 0, DV),
        small[:16, :width].T,
        small[:16, width:],
        small[16, width:],
        beside(out_halves, DV, 2 * DV),
        small[17, width:],
        beside(out_halves, 0, DV).T,
        small[17, :width],
        jnp.concatenate(gate_halves, axis=1),
        jnp.concatenate(up_halves, axis=1),
        jnp.concatenate(down_halves, axis=1).T,
    )


def solution(mesh):
    return jax.shard_map(
        shards,
        mesh=mesh,
        in_specs=(
            P("seq", None),
            P("seq", None),
            P(),
            P(),
            P(),
            P("seq", "head"),
            P("seq", "head"),
            P("seq", "head"),
            P(),
            P(None, "head"),
            P("head"),
            P("seq", "head"),
            P(),
            P("head", "seq"),
            P(),
            P("seq", "head"),
            P("seq", "head"),
            P("head", "seq"),
        ),
        out_specs=(
            P("seq", None),
            P("seq", None),
            P(),
            P("seq", "head"),
            P("seq", "head"),
            P("seq", "head"),
            P(),
            P(None, "head"),
            P("head"),
            P("seq", "head"),
            P(),
            P("head", "seq"),
            P(),
            P("seq", "head"),
            P("seq", "head"),
            P("head", "seq"),
        ),
        check_vma=False,
    )
```
